512 devices in a mesh: prow: 16 (over x, y), pcol: 32 (over z, core).
Axes of the slice: x: 4, y: 4, z: 16, core: 2. Of those that a mesh axis runs over, the one named last changes fastest.
Arguments:
- a_matrix: float32 [16384, 8192], P('prow', 'pcol'), as said below
- row_perms: int32 [2, 128], replicated, may hold values from 0 to 127, each once within a row
- dest_rows: int32 [2, 128], replicated, may hold values from 0 to 127, as said below
- row_mask: int32 [2, 128], replicated, may hold values 0 or 1
- col_mask: int32 [2, 64], replicated, may hold values 0 or 1
Outputs:
- schur_out: float32 [16384, 8192], P('prow', 'pcol')
- l_panels: float32 [16384, 256], P('prow')
The draws below stay inside these ranges and needn't reach their ends.
Inputs may be any that keep to these rules, and one draw needn't show every extreme that they name: `a_matrix`: the two leading diagonal blocks of the window carry 16 sqrt(128) on their diagonal, on top of entries of order one. `dest_rows`: for each section, a permutation of the 128 block rows that keeps a block row's position among the 8 block rows of its device; block rows of one device whose positions differ by less than 16 go to different devices.
All inputs are finite; a program needn't handle non-finite values.
Results may differ from the reference program's by a relative error of at most 0.0001.
Values sent between devices are 32-bit elements; how exact they have to be, the bound alone decides.
No kernel may reach another device: no remote copies, remote signals or barrier semaphores. Data moves between devices by JAX's collectives and lax.ppermute only.
A program may use at most 64 MiB of HBM per device.

```python
import math
import jax
import jax.numpy as jnp
from jax import lax

PANEL = 128
ROW_BLOCKS_DEV = 8
SWEEPS = 3
ROW_BLOCKS = 128
COL_BLOCKS = 64


def draw_a_matrix(key, part):
    shape = (ROW_BLOCKS * PANEL, COL_BLOCKS * PANEL)
    base = jnp.clip(jax.random.normal(key, shape, jnp.float32), -6.0, 6.0)
    row_idx = lax.broadcasted_iota(jnp.int32, shape, 0)
    col_idx = lax.broadcasted_iota(jnp.int32, shape, 1)
    pivot = ((row_idx == col_idx) & (row_idx < 2 * PANEL)).astype(jnp.float32)
    return base + pivot * (16.0 * math.sqrt(PANEL))


def draw_dest_rows(key, part):
    n_dev = ROW_BLOCKS // ROW_BLOCKS_DEV
    owners = jnp.arange(n_dev, dtype=jnp.int32)
    slots = jnp.arange(ROW_BLOCKS_DEV, dtype=jnp.int32)
    result = []
    for section in range(2):
        sigma = jax.random.permutation(jax.random.fold_in(key, 11 + section), n_dev).astype(jnp.int32)
        target_dev = sigma[(owners[:, None] + slots[None, :]) % n_dev]
        result.append((target_dev * ROW_BLOCKS_DEV + slots[None, :]).reshape(-1))
    return jnp.stack(result).astype(jnp.int32)


def place_ends(array, rng, low, top_value):
    spot = [jax.random.randint(jax.random.fold_in(rng, axis), (), 0, length) for axis, length in enumerate(array.shape)]
    longest = array.shape.index(max(array.shape))
    neighbour = spot[:longest] + [(spot[longest] + 1) % array.shape[longest]] + spot[longest + 1:]
    return array.at[tuple(spot)].set(low).at[tuple(neighbour)].set(top_value)


def setup_inputs(seed: int = 0) -> dict:
    keys = jax.random.split(jax.random.key(seed), 6)
    a_matrix = draw_a_matrix(jax.random.fold_in(keys[5], 71), 0)
    row_perms = jax.vmap(lambda own: jax.random.permutation(own, PANEL))(jax.random.split(keys[1], 2)).reshape((2, PANEL)).astype(jnp.int32)
    dest_rows = draw_dest_rows(jax.random.fold_in(keys[5], 71), 0)
    row_mask = place_ends((jax.random.randint(keys[3], (2, ROW_BLOCKS), 0, 4) < 3).astype(jnp.int32), jax.random.fold_in(keys[3], 1), 0, 1)
    col_mask = place_ends((jax.random.randint(keys[4], (2, COL_BLOCKS), 0, 4) < 3).astype(jnp.int32), jax.random.fold_in(keys[4], 1), 0, 1)
    return dict(a_matrix=a_matrix, row_perms=row_perms, dest_rows=dest_rows, row_mask=row_mask, col_mask=col_mask)


def refine(pivot_block):
    width = pivot_block.shape[0]
    identity = jnp.eye(width, dtype=pivot_block.dtype)
    scale = width * (jnp.mean(pivot_block * pivot_block) + 1e-6)
    approx = pivot_block.T / scale
    for sweep in range(SWEEPS):
        inner = jnp.dot(pivot_block, approx, precision=lax.Precision.HIGHEST)
        approx = jnp.dot(approx, 2.0 * identity - inner, precision=lax.Precision.HIGHEST)
    return approx


def reference(a_matrix, row_perms, dest_rows, row_mask, col_mask):
    current = a_matrix
    panels = []
    row_ids = jnp.arange(ROW_BLOCKS, dtype=jnp.int32)
    col_ids = jnp.arange(COL_BLOCKS, dtype=jnp.int32)
    for section in range(2):
        first = section * PANEL
        last = first + PANEL
        upper = current[first:last][row_perms[section]]
        current = current.at[first:last].set(upper)
        inverse = refine(upper[:, first:last])
        row_flags = ((row_mask[section] == 1) & (row_ids > section)).astype(current.dtype)
        lower = jnp.dot(current[:, first:last], inverse, precision=lax.Precision.HIGHEST)
        lower = lower * jnp.repeat(row_flags, PANEL)[:, None]
        panels.append(lower)
        col_flags = ((col_mask[section] == 1) & (col_ids > section)).astype(current.dtype)
        kept = upper * jnp.repeat(col_flags, PANEL)[None, :]
        product = jnp.dot(lower, kept, precision=lax.Precision.HIGHEST)
        blocks = product.reshape(ROW_BLOCKS, PANEL, COL_BLOCKS * PANEL)
        moved = jnp.zeros_like(blocks).at[dest_rows[section]].set(blocks)
        current = current - moved.reshape(ROW_BLOCKS * PANEL, COL_BLOCKS * PANEL)
    return current, jnp.concatenate(panels, axis=1)
```

```python
import jax
import jax.numpy as jnp
from jax import lax
from jax.experimental import pallas as pl
from jax.experimental.pallas import tpu as pltpu
from jax.sharding import Mesh
from jax.sharding import PartitionSpec as P

SWEEPS = 3
W = 128
NP = 16
NZ = 16
HI = lax.Precision.HIGHEST


def dot(a, b):
    return jnp.dot(a, b, precision=HI, preferred_element_type=jnp.float32)


def refine(pivot):
    row = lax.broadcasted_iota(jnp.int32, (W, W), 0)
    col = lax.broadcasted_iota(jnp.int32, (W, W), 1)
    two = jnp.where(row == col, 2.0, 0.0).astype(jnp.float32)
    scale = W * (jnp.mean(pivot * pivot) + 1e-6)
    approx = pivot.T / scale
    for _ in range(SWEEPS):
        approx = dot(approx, two - dot(pivot, approx))
    return approx


def route_kernel(meta, share, passed, half, out):
    core = meta[0]
    kept = meta[5] == 1
    out[...] = jnp.zeros_like(out)
    for j in range(4):
        block = jnp.where(kept, jnp.where(core == 0, share[j, 0], share[j, 1]), passed[j])
        half[j] = block[:, :W]
        half[4 + j] = block[:, W:]
        out[meta[48 + 2 * j + core], 0] = block[:, :W]
        if j == 0:
            out[:, 1] = jnp.broadcast_to(block[None, :, :W], (NP, 8, W))
            out[:, 2] = jnp.broadcast_to(block[None, :, W:], (NP, 8, W))


def pack_kernel(meta, half, got, out):
    core = meta[0]
    out[:8] = half[...]
    for j in range(4):
        out[8 + j] = got[meta[56 + 2 * j + core], 0]
    out[12] = jnp.where(core == 0, got[0, 1], got[meta[4], 1])
    out[13] = got[0, 2]


def factor_kernel(meta, own, oth, perm, lpan, plow, send, lsrc):
    core = meta[0]
    first = core == 0

    def tile(ref, t):
        return ref[:, t].reshape(W, W)

    def even(t):
        return jnp.where(first, tile(own, t), tile(oth, t))

    def odd(t):
        return jnp.where(first, tile(oth, t), tile(own, t))

    def flag(i):
        return meta[i].astype(jnp.float32)

    inv0 = refine(dot(perm[0], even(12)))
    kept01 = dot(perm[0], even(13)) * flag(2)
    low_src = dot(odd(12), inv0) * flag(3)
    lsrc[...] = low_src
    inv1 = refine(dot(perm[1], odd(13) - dot(low_src, kept01)))
    for ref, parity in ((own, core), (oth, 1 - core)):
        col0 = jnp.concatenate([tile(ref, j) for j in range(4)], axis=0)
        ext0 = jnp.concatenate([tile(ref, 8 + j) for j in range(4)], axis=0)
        col1 = jnp.concatenate([tile(ref, 4 + j) for j in range(4)], axis=0)
        low0 = dot(col0, inv0)
        ext0 = dot(ext0, inv0)
        ext0 = jnp.concatenate(
            [ext0[j * W : (j + 1) * W] * flag(24 + 2 * j + parity) for j in range(4)], axis=0
        )
        low1 = dot(col1 - dot(ext0, kept01), inv1)
        for j in range(4):
            slot = 2 * j + parity
            here = pl.ds(pl.multiple_of(slot * W, W), W)
            part = slice(j * W, (j + 1) * W)
            lpan[here, :W] = low0[part] * flag(8 + slot)
            lpan[here, W:] = low1[part] * flag(16 + slot)
            plow[here, :] = ext0[part]
    for slot in range(8):
        half = pl.ds(pl.multiple_of(slot * W + core * (W // 2), W // 2), W // 2)
        send[meta[32 + slot]] = lpan[half, W:]


def first_kernel(meta, a, rows, plow, lsrc, perm, flags, cur, kept):
    up0 = dot(perm[0], rows[:W])
    kept0 = up0 * flags[0:1]
    up1 = dot(perm[1], rows[W:] - dot(lsrc[...], kept0))
    kept[...] = up1 * flags[1:2]
    prod = dot(plow[...], kept0)
    cur[...] = a[...] - prod

    @pl.when(meta[1] == 1)
    def _():
        cur[:W] = up0 - prod[:W]
        cur[W : 2 * W] = up1


def second_kernel(meta, cur, own, oth, kept, out, low):
    core = meta[0]
    h = W // 2
    for slot in range(8):
        dev = meta[40 + slot]
        low[pl.ds(pl.multiple_of(slot * W + core * h, h), h), :] = own[dev]
        low[pl.ds(pl.multiple_of(slot * W + (1 - core) * h, h), h), :] = oth[dev]
    out[...] = cur[...] - dot(low[...], kept[...])


def f32(*shape):
    return jax.ShapeDtypeStruct(shape, jnp.float32)


def call(kernel, out_shape, n_in, scratch=(), flops=0, moved=0):
    smem = pl.BlockSpec(memory_space=pltpu.SMEM)
    vmem = pl.BlockSpec(memory_space=pltpu.VMEM)
    multi = isinstance(out_shape, (tuple, list))
    return pl.pallas_call(
        kernel,
        out_shape=out_shape,
        in_specs=[smem] + [vmem] * n_in,
        out_specs=[vmem] * len(out_shape) if multi else vmem,
        scratch_shapes=list(scratch),
        compiler_params=pltpu.CompilerParams(vmem_limit_bytes=40 * 2**20),
        cost_estimate=pl.CostEstimate(flops=flops, bytes_accessed=moved, transcendentals=0),
    )


def pick(parts, index):
    return lax.dynamic_index_in_dim(parts, index, 0, keepdims=False)


def shards(a, row_perms, dest_rows, row_mask, col_mask):
    me = lax.axis_index("prow")
    z = lax.axis_index("z")
    core = lax.axis_index("core")
    ids = jnp.arange(W, dtype=jnp.int32)
    slots = jnp.arange(8, dtype=jnp.int32)

    src_rows = jnp.sum(
        jnp.where(dest_rows[:, :, None] == ids[None, None, :], ids[None, :, None], 0), axis=1
    )
    row_ok = ((row_mask == 1) & (ids[None, :] > jnp.arange(2, dtype=jnp.int32)[:, None])).astype(jnp.int32)

    def mine(v):
        return lax.dynamic_slice_in_dim(v, me * 8, 8)

    dest_dev0 = mine(dest_rows[0]) // 8
    dest_dev1 = mine(dest_rows[1]) // 8
    src0 = mine(src_rows[0])
    src_dev1 = mine(src_rows[1]) // 8
    head_src = src_rows[0, 1]
    meta = jnp.concatenate(
        [
            jnp.stack(
                [
                    core,
                    (me == 0).astype(jnp.int32),
                    (col_mask[0, 1] == 1).astype(jnp.int32),
                    row_ok[0, head_src],
                    head_src // 8,
                    (core == (z >= 8)).astype(jnp.int32),
                    *[jnp.int32(0)] * 2,
                ]
            ).astype(jnp.int32),
            mine(row_ok[0]),
            mine(row_ok[1]),
            row_ok[0][src0],
            dest_dev1,
            src_dev1,
            dest_dev0,
            src0 // 8,
        ]
    )
    perm = (row_perms[:, :, None] == ids[None, None, :]).astype(jnp.float32)
    col_ids = (z * 2 + core) * 2 + jnp.arange(2, dtype=jnp.int32)
    col_ok = (lax.dynamic_slice_in_dim(col_mask, col_ids[0], 2, axis=1) == 1) & (
        col_ids[None, :] > jnp.arange(2, dtype=jnp.int32)[:, None]
    )
    flags = jnp.repeat(col_ok.astype(jnp.float32), W, axis=1)
    flags = jnp.concatenate([flags, jnp.zeros((6, 2 * W), jnp.float32)], axis=0)

    cut = a.reshape(8, NZ, 8, 2 * W).transpose(1, 0, 2, 3)
    over = lax.ppermute(cut[8:], "core", [(0, 1)])
    chunks = jnp.where(core == 0, cut[:8], over)
    share = jnp.where((z == 0) & (core == 0), chunks[0], jnp.zeros_like(chunks[0]))
    for k in range(8):
        pairs = [(1, 2 * (8 + k) + 1)] + ([(0, 2 * k)] if k else [])
        share = share + lax.ppermute(chunks[k], ("z", "core"), pairs)
    share = share.reshape(4, 2, 8, 2 * W)
    passed = lax.ppermute(pick(share.transpose(1, 0, 2, 3), 1 - core), "core", [(0, 1), (1, 0)])

    rows = a[: 2 * W]
    for step in (8, 4, 2, 1):
        pairs = [(p, p + step) for p in range(0, NP, 2 * step)]
        got = lax.ppermute(rows, "prow", pairs)
        rows = jnp.where(me % (2 * step) == step, got, rows)

    half, out0 = call(route_kernel, (f32(8, 8, W), f32(NP, 3, 8, W)), 2, moved=2**19)(meta, share, passed)
    got0 = lax.all_to_all(out0, "prow", 0, 0, tiled=True)
    payload = call(pack_kernel, f32(14, 8, W), 2, moved=2**19)(meta, half, got0)

    own = lax.all_gather(payload, "z", axis=0, tiled=False)
    oth = lax.ppermute(own, "core", [(0, 1), (1, 0)])

    lpan, plow, send, lsrc = call(
        factor_kernel,
        (f32(8 * W, 2 * W), f32(8 * W, W), f32(NP, W // 2, W), f32(W, W)),
        3,
        flops=5 * 10**8,
        moved=4 * 2**20,
    )(meta, own, oth, perm)

    got1 = lax.all_to_all(send, "prow", 0, 0, tiled=True)
    cur, kept = call(
        first_kernel, (f32(8 * W, 2 * W), f32(W, 2 * W)), 6, flops=5 * 10**8, moved=3 * 2**20
    )(meta, a, rows, plow, lsrc, perm, flags)
    oth1 = lax.ppermute(got1, "core", [(0, 1), (1, 0)])
    schur = call(
        second_kernel,
        f32(8 * W, 2 * W),
        4,
        scratch=(pltpu.VMEM((8 * W, W), jnp.float32),),
        flops=5 * 10**8,
        moved=3 * 2**20,
    )(meta, cur, got1, oth1, kept)
    return schur, lpan


def solution(mesh):
    fine = Mesh(mesh.devices.reshape(NP, NZ, 2), ("prow", "z", "core"))
    placed = (P("prow", ("z", "core")), P(), P(), P(), P())
    return jax.shard_map(
        shards,
        mesh=fine,
        in_specs=placed,
        out_specs=(P("prow", ("z", "core")), P("prow", None)),
        check_vma=False,
    )
```

```python
import jax
import jax.numpy as jnp
from jax import lax
from jax.experimental import pallas as pl
from jax.experimental.pallas import tpu as pltpu
from jax.sharding import Mesh
from jax.sharding import PartitionSpec as P

SWEEPS = 3
W = 128
NP = 16
NZ = 16
HI = lax.Precision.HIGHEST


def dot(a, b):
    return jnp.dot(a, b, precision=HI, preferred_element_type=jnp.float32)


def order(perms, k):
    hit = lax.broadcasted_iota(jnp.int32, (W, W), 0) == perms[k : k + 1, :]
    return jnp.where(hit, 1.0, 0.0).astype(jnp.float32).T


def refine(pivot):
    row = lax.broadcasted_iota(jnp.int32, (W, W), 0)
    col = lax.broadcasted_iota(jnp.int32, (W, W), 1)
    two = jnp.where(row == col, 2.0, 0.0).astype(jnp.float32)
    scale = W * (jnp.mean(pivot * pivot) + 1e-6)
    approx = pivot.T / scale
    for _ in range(SWEEPS):
        approx = dot(approx, two - dot(pivot, approx))
    return approx


def index_kernel(dest, row_mask, col_mask, meta, src):
    me = lax.axis_index("x") * 4 + lax.axis_index("y")
    z = lax.axis_index("z")
    core = lax.axis_index("core")

    def invert(i, carry):
        src[0, dest[0, i]] = i
        src[1, dest[1, i]] = i
        return carry

    lax.fori_loop(0, W, invert, 0, unroll=8)

    def row_ok(k, i):
        return ((row_mask[k, i] == 1) & (i > k)).astype(jnp.int32)

    def col_ok(k, j):
        return ((col_mask[k, j] == 1) & (j > k)).astype(jnp.int32)

    head = src[0, 1]
    block = (z * 2 + core) * 2
    meta[0] = core
    meta[1] = (me == 0).astype(jnp.int32)
    meta[2] = col_ok(0, 1)
    meta[3] = row_ok(0, head)
    meta[4] = lax.shift_right_logical(head, 3)
    meta[5] = (core == (z >= 8).astype(jnp.int32)).astype(jnp.int32)
    for k in range(2):
        for j in range(2):
            meta[64 + 2 * k + j] = col_ok(k, block + j)
    for slot in range(8):
        here = me * 8 + slot
        meta[8 + slot] = row_ok(0, here)
        meta[16 + slot] = row_ok(1, here)
        meta[24 + slot] = row_ok(0, src[0, here])
        meta[32 + slot] = lax.shift_right_logical(dest[1, here], 3)
        meta[40 + slot] = lax.shift_right_logical(src[1, here], 3)
        meta[48 + slot] = lax.shift_right_logical(dest[0, here], 3)
        meta[56 + slot] = lax.shift_right_logical(src[0, here], 3)


def route_kernel(meta, share, passed, half, out):
    core = meta[0]
    kept = meta[5] == 1
    out[...] = jnp.zeros_like(out)
    for j in range(4):
        block = jnp.where(kept, jnp.where(core == 0, share[j, 0], share[j, 1]), passed[j])
        half[j] = block[:, :W]
        half[4 + j] = block[:, W:]
        out[meta[48 + 2 * j + core], 0] = block[:, :W]
        if j == 0:
            out[:, 1] = jnp.broadcast_to(block[None, :, :W], (NP, 8, W))
            out[:, 2] = jnp.broadcast_to(block[None, :, W:], (NP, 8, W))


def pack_kernel(meta, half, got, out):
    core = meta[0]
    out[:8] = half[...]
    for j in range(4):
        out[8 + j] = got[meta[56 + 2 * j + core], 0]
    out[12] = jnp.where(core == 0, got[0, 1], got[meta[4], 1])
    out[13] = got[0, 2]


def factor_kernel(meta, own, oth, perms, lpan, plow, send, lsrc):
    core = meta[0]
    first = core == 0

    def tile(ref, t):
        return ref[:, t].reshape(W, W)

    def even(t):
        return jnp.where(first, tile(own, t), tile(oth, t))

    def odd(t):
        return jnp.where(first, tile(oth, t), tile(own, t))

    def flag(i):
        return meta[i].astype(jnp.float32)

    inv0 = refine(dot(order(perms, 0), even(12)))
    kept01 = dot(order(perms, 0), even(13)) * flag(2)
    low_src = dot(odd(12), inv0) * flag(3)
    lsrc[...] = low_src
    inv1 = refine(dot(order(perms, 1), odd(13) - dot(low_src, kept01)))
    for ref, parity in ((own, core), (oth, 1 - core)):
        col0 = jnp.concatenate([tile(ref, j) for j in range(4)], axis=0)
        ext0 = jnp.concatenate([tile(ref, 8 + j) for j in range(4)], axis=0)
        col1 = jnp.concatenate([tile(ref, 4 + j) for j in range(4)], axis=0)
        low0 = dot(col0, inv0)
        ext0 = dot(ext0, inv0)
        ext0 = jnp.concatenate(
            [ext0[j * W : (j + 1) * W] * flag(24 + 2 * j + parity) for j in range(4)], axis=0
        )
        low1 = dot(col1 - dot(ext0, kept01), inv1)
        for j in range(4):
            slot = 2 * j + parity
            here = pl.ds(pl.multiple_of(slot * W, W), W)
            part = slice(j * W, (j + 1) * W)
            lpan[here, :W] = low0[part] * flag(8 + slot)
            lpan[here, W:] = low1[part] * flag(16 + slot)
            plow[here, :] = ext0[part]
    for slot in range(8):
        half = pl.ds(pl.multiple_of(slot * W + core * (W // 2), W // 2), W // 2)
        send[meta[32 + slot]] = lpan[half, W:]


def first_kernel(meta, a, rows, plow, lsrc, perms, cur, kept):
    def masked(block, k):
        return jnp.concatenate(
            [block[:, j * W : (j + 1) * W] * meta[64 + 2 * k + j].astype(jnp.float32) for j in range(2)],
            axis=1,
        )

    up0 = dot(order(perms, 0), rows[:W])
    kept0 = masked(up0, 0)
    up1 = dot(order(perms, 1), rows[W:] - dot(lsrc[...], kept0))
    kept[...] = masked(up1, 1)
    prod = dot(plow[...], kept0)
    cur[...] = a[...] - prod

    @pl.when(meta[1] == 1)
    def _():
        cur[:W] = up0 - prod[:W]
        cur[W : 2 * W] = up1


def second_kernel(meta, cur, own, oth, kept, out, low):
    core = meta[0]
    h = W // 2
    for slot in range(8):
        dev = meta[40 + slot]
        low[pl.ds(pl.multiple_of(slot * W + core * h, h), h), :] = own[dev]
        low[pl.ds(pl.multiple_of(slot * W + (1 - core) * h, h), h), :] = oth[dev]
    out[...] = cur[...] - dot(low[...], kept[...])


def f32(*shape):
    return jax.ShapeDtypeStruct(shape, jnp.float32)


def call(kernel, out_shape, n_in, scratch=(), flops=0, moved=0):
    smem = pl.BlockSpec(memory_space=pltpu.SMEM)
    vmem = pl.BlockSpec(memory_space=pltpu.VMEM)
    multi = isinstance(out_shape, (tuple, list))
    return pl.pallas_call(
        kernel,
        out_shape=out_shape,
        in_specs=[smem] + [vmem] * n_in,
        out_specs=[vmem] * len(out_shape) if multi else vmem,
        scratch_shapes=list(scratch),
        compiler_params=pltpu.CompilerParams(vmem_limit_bytes=16 * 2**20),
        cost_estimate=pl.CostEstimate(flops=flops, bytes_accessed=moved, transcendentals=0),
    )


def shards(a, row_perms, dest_rows, row_mask, col_mask):
    z = lax.axis_index("z")
    core = lax.axis_index("core")
    smem = pl.BlockSpec(memory_space=pltpu.SMEM)
    meta = pl.pallas_call(
        index_kernel,
        out_shape=jax.ShapeDtypeStruct((W,), jnp.int32),
        in_specs=[smem] * 3,
        out_specs=smem,
        scratch_shapes=[pltpu.SMEM((2, W), jnp.int32)],
    )(dest_rows, row_mask, col_mask)

    rows = lax.all_gather(a[: 2 * W], "x", axis=0, tiled=True)[: 2 * W]

    cut = a.reshape(8, NZ, 8, 2 * W)
    over = lax.ppermute(cut[:, 8:].transpose(1, 0, 2, 3), "core", [(0, 1)])
    pieces = [jnp.where(core == 0, cut[:, step % 8], over[8 - step]) for step in range(1, 9)]
    pieces, meta = lax.optimization_barrier((pieces, meta))
    share = jnp.where((z == 0) & (core == 0), pieces[7], jnp.zeros_like(pieces[7]))
    for step in range(1, 9):
        pairs = [(1, 2 * (NZ - step) + 1)]
        if step < 8:
            pairs.append((0, 2 * step))
        share = share + lax.ppermute(pieces[step - 1], ("z", "core"), pairs)
    share = share.reshape(4, 2, 8, 2 * W)
    passed = lax.ppermute(
        lax.dynamic_index_in_dim(share, 1 - core, 1, keepdims=False), "core", [(0, 1), (1, 0)]
    )

    half, out0 = call(route_kernel, (f32(8, 8, W), f32(NP, 3, 8, W)), 2, moved=2**19)(meta, share, passed)
    got0 = lax.all_to_all(out0, ("x", "y"), 0, 0, tiled=True)
    payload = call(pack_kernel, f32(14, 8, W), 2, moved=2**19)(meta, half, got0)

    payload, rows = lax.optimization_barrier((payload, rows))
    rows = lax.all_gather(rows, "y", axis=0, tiled=True)[: 2 * W]
    own = lax.all_gather(payload, "z", axis=0, tiled=False)
    oth = lax.ppermute(own, "core", [(0, 1), (1, 0)])
    oth, rows = lax.optimization_barrier((oth, rows))

    lpan, plow, send, lsrc = call(
        factor_kernel,
        (f32(8 * W, 2 * W), f32(8 * W, W), f32(NP, W // 2, W), f32(W, W)),
        3,
        flops=5 * 10**8,
        moved=4 * 2**20,
    )(meta, own, oth, row_perms)

    got1 = lax.all_to_all(send, ("x", "y"), 0, 0, tiled=True)
    cur, kept = call(
        first_kernel, (f32(8 * W, 2 * W), f32(W, 2 * W)), 5, flops=5 * 10**8, moved=3 * 2**20
    )(meta, a, rows, plow, lsrc, row_perms)
    oth1 = lax.ppermute(got1, "core", [(0, 1), (1, 0)])
    schur = call(
        second_kernel,
        f32(8 * W, 2 * W),
        4,
        scratch=(pltpu.VMEM((8 * W, W), jnp.float32),),
        flops=5 * 10**8,
        moved=3 * 2**20,
    )(meta, cur, got1, oth1, kept)
    return schur, lpan


def solution(mesh):
    fine = Mesh(mesh.devices.reshape(4, 4, NZ, 2), ("x", "y", "z", "core"))
    placed = (P(("x", "y"), ("z", "core")), P(), P(), P(), P())
    return jax.shard_map(
        shards,
        mesh=fine,
        in_specs=placed,
        out_specs=(P(("x", "y"), ("z", "core")), P(("x", "y"), None)),
        check_vma=False,
    )
```

```python
import jax
import jax.numpy as jnp
from jax import lax
from jax.experimental import pallas as pl
from jax.experimental.pallas import tpu as pltpu
from jax.sharding import Mesh
from jax.sharding import PartitionSpec as P

SWEEPS = 3
W = 128
H = W // 2
NP = 16
NZ = 16
SLOTS = 8


def split(x):
    high = x.astype(jnp.bfloat16)
    rest = x - high.astype(jnp.float32)
    mid = rest.astype(jnp.bfloat16)
    low = (rest - mid.astype(jnp.float32)).astype(jnp.bfloat16)
    return high, mid, low


def dot16(a, b):
    return jnp.dot(a, b, preferred_element_type=jnp.float32)


def dot(a, b):
    ah, am, al = split(a)
    bh, bm, bl = split(b)
    lead = jnp.concatenate([ah, am], axis=1)
    tail = jnp.concatenate([ah, al], axis=1)
    right = jnp.concatenate([bh, bm], axis=1)
    first = dot16(lead, jnp.concatenate([right, right], axis=0))
    second = dot16(tail, jnp.concatenate([bl, bh], axis=0))
    n = b.shape[1]
    return first[:, :n] + (first[:, n:] + second)


def index_kernel(dest, row_mask, col_mask, meta, src):
    me = lax.axis_index("x") * 4 + lax.axis_index("y")
    z = lax.axis_index("z")
    core = lax.axis_index("core")

    def invert(i, carry):
        src[0, dest[0, i]] = i
        src[1, dest[1, i]] = i
        return carry

    lax.fori_loop(0, W, invert, 0, unroll=8)

    def row_ok(k, i):
        return ((row_mask[k, i] == 1) & (i > k)).astype(jnp.int32)

    def col_ok(k, j):
        return ((col_mask[k, j] == 1) & (j > k)).astype(jnp.int32)

    head = src[0, 1]
    block = (z * 2 + core) * 2
    meta[0] = core
    meta[1] = (me == 0).astype(jnp.int32)
    meta[2] = col_ok(0, 1)
    meta[3] = row_ok(0, head)
    meta[4] = lax.shift_right_logical(head, 3)
    meta[5] = ((z == 0) & (core == 0)).astype(jnp.int32)
    for k in range(2):
        for j in range(2):
            meta[64 + 2 * k + j] = col_ok(k, block + j)
    for slot in range(SLOTS):
        here = me * SLOTS + slot
        meta[8 + slot] = row_ok(0, here)
        meta[16 + slot] = row_ok(1, here)
        meta[24 + slot] = row_ok(0, src[0, here])
        meta[32 + slot] = lax.shift_right_logical(dest[1, here], 3)
        meta[40 + slot] = lax.shift_right_logical(src[1, here], 3)
        meta[48 + slot] = lax.shift_right_logical(dest[0, here], 3)
        meta[56 + slot] = lax.shift_right_logical(src[0, here], 3)


def route_kernel(meta, a, own, *refs):
    got, (out, panel, last) = refs[:-3], refs[-3:]
    share = own[...] * meta[5].astype(jnp.float32)
    for ref in got:
        share = share + ref[...]
    out[...] = jnp.zeros_like(out)
    for slot in range(SLOTS):
        left, right = share[slot, :, :W], share[slot, :, W:]
        out[meta[48 + slot], 0] = left
        if slot < 7:
            panel[slot] = left
            panel[7 + slot] = right
        else:
            last[0] = left
            last[1] = right
        if slot < 2:
            out[:, 1 + 2 * slot] = jnp.broadcast_to(left[None], (NP, 8, W))
            out[:, 2 + 2 * slot] = jnp.broadcast_to(right[None], (NP, 8, W))
    rows = a[: 2 * W].reshape(NP, 2, 8, 2 * W)
    out[:, 5:7] = rows[..., :W]
    out[:, 7:9] = rows[..., W:]


def pack_kernel(meta, passed, last, got, out, chunk):
    chunk[...] = got[0, 5:9]

    @pl.when(meta[0] == 1)
    def _():
        out[...] = passed[...]

    @pl.when(meta[0] == 0)
    def _():
        out[:2] = last[...]
        for slot in range(SLOTS):
            out[2 + slot] = got[meta[56 + slot], 0]
        out[10:12] = got[0, 1:3]
        out[12] = got[meta[4], 3]
        out[13] = got[0, 4]


def order(perms, k):
    hit = lax.broadcasted_iota(jnp.int32, (W, W), 0) == perms[k : k + 1, :]
    return jnp.where(hit, 1.0, 0.0).astype(jnp.float32).T


def refine(pivot):
    row = lax.broadcasted_iota(jnp.int32, (W, W), 0)
    col = lax.broadcasted_iota(jnp.int32, (W, W), 1)
    two = jnp.where(row == col, 2.0, 0.0).astype(jnp.float32)
    scale = W * (jnp.mean(pivot * pivot) + 1e-6)
    approx = pivot.T / scale
    for _ in range(SWEEPS):
        approx = dot(approx, two - dot(pivot, approx))
    return approx


def factor(meta, head, panel, chunk, perms, lpan, plow, send, lsrc):
    def tile(ref, t):
        return ref[:, t].reshape(W, W)

    def flag(i):
        return meta[i].astype(jnp.float32)

    def flagged(block, base):
        return jnp.concatenate(
            [block[s * W : (s + 1) * W] * flag(base + s) for s in range(SLOTS)], axis=0
        )

    inv0 = refine(dot(order(perms, 0), tile(head, 10)))
    kept01 = dot(order(perms, 0), tile(head, 11)) * flag(2)
    low_src = dot(tile(head, 12), inv0) * flag(3)
    lsrc[...] = low_src
    inv1 = refine(dot(order(perms, 1), tile(head, 13) - dot(low_src, kept01)))
    col0 = jnp.concatenate([tile(panel, s) for s in range(7)] + [tile(head, 0)], axis=0)
    lpan[:, :W] = flagged(dot(col0, inv0), 8)
    ext0 = jnp.concatenate([tile(head, 2 + s) for s in range(SLOTS)], axis=0)
    ext0 = flagged(dot(ext0, inv0), 24)
    plow[...] = ext0
    col1 = jnp.concatenate([tile(panel, 7 + s) for s in range(7)] + [tile(head, 1)], axis=0)
    lpan[:, W:] = flagged(dot(col1 - dot(ext0, kept01), inv1), 16)
    for slot in range(SLOTS):
        half = pl.ds(pl.multiple_of(slot * W + meta[0] * H, H), H)
        send[meta[32 + slot], :H] = lpan[half, W:]
    send[:, H:] = jnp.broadcast_to(chunk[...].reshape(1, 32, W), (NP, 32, W))


def factor_kernel(meta, own, oth, *refs):
    @pl.when(meta[0] == 0)
    def _():
        factor(meta, own, oth, *refs)

    @pl.when(meta[0] == 1)
    def _():
        factor(meta, oth, own, *refs)


def first_kernel(meta, a, got, plow, lsrc, perms, cur, kept):
    def masked(block, k):
        return jnp.concatenate(
            [block[:, j * W : (j + 1) * W] * meta[64 + 2 * k + j].astype(jnp.float32) for j in range(2)],
            axis=1,
        )

    rows = jnp.concatenate(
        [got[:, H : H + 16].reshape(2 * W, W), got[:, H + 16 :].reshape(2 * W, W)], axis=1
    )
    up0 = dot(order(perms, 0), rows[:W])
    kept0 = masked(up0, 0)
    up1 = dot(order(perms, 1), rows[W:] - dot(lsrc[...], kept0))
    kept[...] = masked(up1, 1)
    prod = dot(plow[...], kept0)
    cur[...] = a[...] - prod

    @pl.when(meta[1] == 1)
    def _():
        cur[:W] = up0 - prod[:W]
        cur[W : 2 * W] = up1


def second_kernel(meta, cur, own, oth, kept, out, low):
    core = meta[0]
    for slot in range(SLOTS):
        dev = meta[40 + slot]
        low[pl.ds(pl.multiple_of(slot * W + core * H, H), H), :] = own[dev, :H]
        low[pl.ds(pl.multiple_of(slot * W + (1 - core) * H, H), H), :] = oth[dev]
    out[...] = cur[...] - dot(low[...], kept[...])


def f32(*shape):
    return jax.ShapeDtypeStruct(shape, jnp.float32)


def call(kernel, out_shape, n_in, scratch=(), flops=0, moved=0):
    smem = pl.BlockSpec(memory_space=pltpu.SMEM)
    vmem = pl.BlockSpec(memory_space=pltpu.VMEM)
    multi = isinstance(out_shape, (tuple, list))
    return pl.pallas_call(
        kernel,
        out_shape=out_shape,
        in_specs=[smem] + [vmem] * n_in,
        out_specs=[vmem] * len(out_shape) if multi else vmem,
        scratch_shapes=list(scratch),
        compiler_params=pltpu.CompilerParams(vmem_limit_bytes=24 * 2**20),
        cost_estimate=pl.CostEstimate(flops=flops, bytes_accessed=moved, transcendentals=0),
    )


def shards(a, row_perms, dest_rows, row_mask, col_mask):
    core = lax.axis_index("core")
    smem = pl.BlockSpec(memory_space=pltpu.SMEM)
    meta = pl.pallas_call(
        index_kernel,
        out_shape=jax.ShapeDtypeStruct((W,), jnp.int32),
        in_specs=[smem] * 3,
        out_specs=smem,
        scratch_shapes=[pltpu.SMEM((2, W), jnp.int32)],
    )(dest_rows, row_mask, col_mask)

    cut = a.reshape(SLOTS, NZ, 8, 2 * W)
    over = lax.ppermute(cut[:, 8:].transpose(1, 0, 2, 3), "core", [(0, 1)])
    pieces = [jnp.where(core == 0, cut[:, step % 8], over[8 - step]) for step in range(1, 9)]
    pieces, meta = lax.optimization_barrier((pieces, meta))
    got = []
    for step in range(1, 9):
        pairs = [(1, 2 * (NZ - step))]
        if step < 8:
            pairs.append((0, 2 * step))
        got.append(lax.ppermute(pieces[step - 1], ("z", "core"), pairs))

    out0, panel, last = call(
        route_kernel, (f32(NP, 9, 8, W), f32(14, 8, W), f32(2, 8, W)), 10, moved=2**20
    )(meta, a[: 2 * W], pieces[7], *got)
    passed = lax.ppermute(panel, "core", [(0, 1)])
    got0 = lax.all_to_all(out0, ("x", "y"), 0, 0, tiled=True)
    payload, chunk = call(pack_kernel, (f32(14, 8, W), f32(4, 8, W)), 3, moved=2**19)(
        meta, passed, last, got0
    )

    own = lax.all_gather(payload, "z", axis=0, tiled=False)
    oth = lax.ppermute(own, "core", [(0, 1), (1, 0)])

    lpan, plow, send, lsrc = call(
        factor_kernel,
        (f32(SLOTS * W, 2 * W), f32(SLOTS * W, W), f32(NP, H + 32, W), f32(W, W)),
        4,
        flops=5 * 10**8,
        moved=4 * 2**20,
    )(meta, own, oth, chunk, row_perms)

    got1 = lax.all_to_all(send, ("x", "y"), 0, 0, tiled=True)
    oth1 = lax.ppermute(got1[:, :H], "core", [(0, 1), (1, 0)])
    cur, kept = call(
        first_kernel, (f32(SLOTS * W, 2 * W), f32(W, 2 * W)), 5, flops=5 * 10**8, moved=3 * 2**20
    )(meta, a, got1, plow, lsrc, row_perms)
    schur = call(
        second_kernel,
        f32(SLOTS * W, 2 * W),
        4,
        scratch=(pltpu.VMEM((SLOTS * W, W), jnp.float32),),
        flops=5 * 10**8,
        moved=3 * 2**20,
    )(meta, cur, got1, oth1, kept)
    return schur, lpan


def solution(mesh):
    fine = Mesh(mesh.devices.reshape(4, 4, NZ, 2), ("x", "y", "z", "core"))
    placed = (P(("x", "y"), ("z", "core")), P(), P(), P(), P())
    return jax.shard_map(
        shards,
        mesh=fine,
        in_specs=placed,
        out_specs=(P(("x", "y"), ("z", "core")), P(("x", "y"), None)),
        check_vma=False,
    )
```

```python
import jax
import jax.numpy as jnp
from jax import lax
from jax.experimental import pallas as pl
from jax.experimental.pallas import tpu as pltpu
from jax.sharding import Mesh
from jax.sharding import PartitionSpec as P

SWEEPS = 3
W = 128
H = W // 2
NP = 16
NZ = 16
SLOTS = 8
SENDS = ((8, 9), (7, 10), (6, 11), (5, 12), (4, 13), (3, 14), (2, 15), (1, 0))


def split(x):
    high = x.astype(jnp.bfloat16)
    rest = x - high.astype(jnp.float32)
    mid = rest.astype(jnp.bfloat16)
    low = (rest - mid.astype(jnp.float32)).astype(jnp.bfloat16)
    return high, mid, low


def dot16(a, b):
    return jnp.dot(a, b, preferred_element_type=jnp.float32)


def dot(a, b):
    ah, am, al = split(a)
    bh, bm, bl = split(b)
    lead = jnp.concatenate([ah, am], axis=1)
    tail = jnp.concatenate([ah, al], axis=1)
    right = jnp.concatenate([bh, bm], axis=1)
    first = dot16(lead, jnp.concatenate([right, right], axis=0))
    second = dot16(tail, jnp.concatenate([bl, bh], axis=0))
    n = b.shape[1]
    return first[:, :n] + (first[:, n:] + second)


def index_kernel(dest, row_mask, col_mask, meta, src):
    me = lax.axis_index("x") * 4 + lax.axis_index("y")
    z = lax.axis_index("z")
    core = lax.axis_index("core")

    def invert(i, carry):
        src[0, dest[0, i]] = i
        src[1, dest[1, i]] = i
        return carry

    lax.fori_loop(0, W, invert, 0, unroll=8)

    def row_ok(k, i):
        return ((row_mask[k, i] == 1) & (i > k)).astype(jnp.int32)

    def col_ok(k, j):
        return ((col_mask[k, j] == 1) & (j > k)).astype(jnp.int32)

    head = src[0, 1]
    block = (z * 2 + core) * 2
    meta[0] = core
    meta[1] = (me == 0).astype(jnp.int32)
    meta[2] = col_ok(0, 1)
    meta[3] = row_ok(0, head)
    meta[4] = lax.shift_right_logical(head, 3)
    meta[5] = ((z == 0) & (core == 0)).astype(jnp.int32)
    for k in range(2):
        for j in range(2):
            meta[64 + 2 * k + j] = col_ok(k, block + j)
    for slot in range(SLOTS):
        here = me * SLOTS + slot
        meta[8 + slot] = row_ok(0, here)
        meta[16 + slot] = row_ok(1, here)
        meta[24 + slot] = row_ok(0, src[0, here])
        meta[32 + slot] = lax.shift_right_logical(dest[1, here], 3)
        meta[40 + slot] = lax.shift_right_logical(src[1, here], 3)
        meta[48 + slot] = lax.shift_right_logical(dest[0, here], 3)
        meta[56 + slot] = lax.shift_right_logical(src[0, here], 3)


def route_kernel(meta, own, *refs):
    got, (out, panel, last) = refs[:-3], refs[-3:]
    share = own[...] * meta[5].astype(jnp.float32)
    for ref in got:
        share = share + ref[...]
    out[...] = jnp.zeros_like(out)
    for slot in range(SLOTS):
        left, right = share[slot, :, :W], share[slot, :, W:]
        out[meta[48 + slot], 0] = left
        if slot < 7:
            panel[slot] = left
            panel[7 + slot] = right
        else:
            last[0] = left
            last[1] = right
        if slot < 2:
            out[:, 1 + 2 * slot] = jnp.broadcast_to(left[None], (NP, 8, W))
            out[:, 2 + 2 * slot] = jnp.broadcast_to(right[None], (NP, 8, W))


def pack_kernel(meta, passed, last, got, out):
    @pl.when(meta[0] == 1)
    def _():
        out[...] = passed[...]

    @pl.when(meta[0] == 0)
    def _():
        out[:2] = last[...]
        for slot in range(SLOTS):
            out[2 + slot] = got[meta[56 + slot], 0]
        out[10:12] = got[0, 1:3]
        out[12] = got[meta[4], 3]
        out[13] = got[0, 4]


def order(perms, k):
    hit = lax.broadcasted_iota(jnp.int32, (W, W), 0) == perms[k : k + 1, :]
    return jnp.where(hit, 1.0, 0.0).astype(jnp.float32).T


def refine(pivot):
    row = lax.broadcasted_iota(jnp.int32, (W, W), 0)
    col = lax.broadcasted_iota(jnp.int32, (W, W), 1)
    two = jnp.where(row == col, 2.0, 0.0).astype(jnp.float32)
    scale = W * (jnp.mean(pivot * pivot) + 1e-6)
    approx = pivot.T / scale
    for _ in range(SWEEPS):
        approx = dot(approx, two - dot(pivot, approx))
    return approx


def factor(meta, head, panel, perms, lpan, plow, send, lsrc, kept):
    def tile(ref, t):
        return ref[:, t].reshape(W, W)

    def flag(i):
        return meta[i].astype(jnp.float32)

    def flagged(block, base):
        return jnp.concatenate(
            [block[s * W : (s + 1) * W] * flag(base + s) for s in range(SLOTS)], axis=0
        )

    inv0 = refine(dot(order(perms, 0), tile(head, 10)))
    kept01 = dot(order(perms, 0), tile(head, 11)) * flag(2)
    low_src = dot(tile(head, 12), inv0) * flag(3)
    lsrc[...] = low_src
    kept[...] = kept01
    inv1 = refine(dot(order(perms, 1), tile(head, 13) - dot(low_src, kept01)))
    col0 = jnp.concatenate([tile(panel, s) for s in range(7)] + [tile(head, 0)], axis=0)
    lpan[:, :W] = flagged(dot(col0, inv0), 8)
    ext0 = jnp.concatenate([tile(head, 2 + s) for s in range(SLOTS)], axis=0)
    ext0 = flagged(dot(ext0, inv0), 24)
    plow[...] = ext0
    col1 = jnp.concatenate([tile(panel, 7 + s) for s in range(7)] + [tile(head, 1)], axis=0)
    lpan[:, W:] = flagged(dot(col1 - dot(ext0, kept01), inv1), 16)
    for slot in range(SLOTS):
        half = pl.ds(pl.multiple_of(slot * W + meta[0] * H, H), H)
        send[meta[32 + slot]] = lpan[half, W:]


def factor_kernel(meta, own, oth, *refs):
    @pl.when(meta[0] == 0)
    def _():
        factor(meta, own, oth, *refs)

    @pl.when(meta[0] == 1)
    def _():
        factor(meta, oth, own, *refs)


def first_kernel(meta, a, rows, plow, lsrc, kept01, perms, cur, kept):
    def masked(block, k):
        return jnp.concatenate(
            [block[:, j * W : (j + 1) * W] * meta[64 + 2 * k + j].astype(jnp.float32) for j in range(2)],
            axis=1,
        )

    up0 = dot(order(perms, 0), rows[:W])
    kept0 = masked(up0, 0)
    right = jnp.where(meta[5] == 1, kept01[...], kept0[:, W:])
    kept0 = jnp.concatenate([kept0[:, :W], right], axis=1)
    up1 = dot(order(perms, 1), rows[W:] - dot(lsrc[...], kept0))
    kept[...] = masked(up1, 1)
    prod = dot(plow[...], kept0)
    cur[...] = a[...] - prod

    @pl.when(meta[1] == 1)
    def _():
        cur[:W] = up0 - prod[:W]
        cur[W : 2 * W] = up1


def second_kernel(meta, cur, own, oth, kept, out, low):
    core = meta[0]
    for slot in range(SLOTS):
        dev = meta[40 + slot]
        low[pl.ds(pl.multiple_of(slot * W + core * H, H), H), :] = own[dev]
        low[pl.ds(pl.multiple_of(slot * W + (1 - core) * H, H), H), :] = oth[dev]
    out[...] = cur[...] - dot(low[...], kept[...])


def f32(*shape):
    return jax.ShapeDtypeStruct(shape, jnp.float32)


def call(kernel, out_shape, n_in, scratch=(), flops=0, moved=0):
    smem = pl.BlockSpec(memory_space=pltpu.SMEM)
    vmem = pl.BlockSpec(memory_space=pltpu.VMEM)
    multi = isinstance(out_shape, (tuple, list))
    return pl.pallas_call(
        kernel,
        out_shape=out_shape,
        in_specs=[smem] + [vmem] * n_in,
        out_specs=[vmem] * len(out_shape) if multi else vmem,
        scratch_shapes=list(scratch),
        compiler_params=pltpu.CompilerParams(vmem_limit_bytes=16 * 2**20),
        cost_estimate=pl.CostEstimate(flops=flops, bytes_accessed=moved, transcendentals=0),
    )


def spread(block, axis):
    names = (axis, "z", "core")
    return [
        lax.ppermute(block, names, [(r, k * 2 * NZ + r) for r in range(1, 2 * NZ)]) for k in range(1, 4)
    ]


def settle(block, copies, index):
    for k in range(1, 4):
        block = jnp.where(index == k, copies[k - 1], block)
    return block


def shards(a, row_perms, dest_rows, row_mask, col_mask):
    core = lax.axis_index("core")
    smem = pl.BlockSpec(memory_space=pltpu.SMEM)
    cut = a.reshape(SLOTS, NZ, 8, 2 * W)
    over = lax.ppermute(cut[:, 9:].transpose(1, 0, 2, 3), ("z", "core"), [(0, 1)])
    got = []
    for z0, z1 in SENDS:
        pairs, piece = [(0, 2 * z0)], cut[:, z0]
        if z1:
            pairs.append((1, 2 * z1))
            piece = jnp.where(core == 0, piece, over[z1 - 9])
        got.append(lax.ppermute(piece, ("z", "core"), pairs))

    got[0], maps = lax.optimization_barrier((got[0], (dest_rows, row_mask, col_mask)))
    meta = pl.pallas_call(
        index_kernel,
        out_shape=jax.ShapeDtypeStruct((W,), jnp.int32),
        in_specs=[smem] * 3,
        out_specs=smem,
        scratch_shapes=[pltpu.SMEM((2, W), jnp.int32)],
    )(*maps)

    out0, panel, last = call(
        route_kernel, (f32(NP, 5, 8, W), f32(14, 8, W), f32(2, 8, W)), 9, moved=2**20
    )(meta, cut[:, 0], *got)
    passed = lax.ppermute(panel, "core", [(0, 1)])
    out0, rows = lax.optimization_barrier((out0, a[: 2 * W]))
    copies = spread(rows, "x")
    got0 = lax.all_to_all(out0, ("x", "y"), 0, 0, tiled=True)
    payload = call(pack_kernel, f32(14, 8, W), 3, moved=2**19)(meta, passed, last, got0)

    payload, copies = lax.optimization_barrier((payload, copies))
    own = lax.all_gather(payload, "z", axis=0, tiled=False)
    oth = lax.ppermute(own, "core", [(0, 1), (1, 0)])

    lpan, plow, send, lsrc, kept01 = call(
        factor_kernel,
        (f32(SLOTS * W, 2 * W), f32(SLOTS * W, W), f32(NP, H, W), f32(W, W), f32(W, W)),
        3,
        flops=5 * 10**8,
        moved=4 * 2**20,
    )(meta, own, oth, row_perms)

    send, copies = lax.optimization_barrier((send, copies))
    rows = settle(rows, copies, lax.axis_index("x"))
    rows = settle(rows, spread(rows, "y"), lax.axis_index("y"))
    got1 = lax.all_to_all(send, ("x", "y"), 0, 0, tiled=True)
    oth1 = lax.ppermute(got1, "core", [(0, 1), (1, 0)])
    cur, kept = call(
        first_kernel, (f32(SLOTS * W, 2 * W), f32(W, 2 * W)), 6, flops=5 * 10**8, moved=3 * 2**20
    )(meta, a, rows, plow, lsrc, kept01, row_perms)
    schur = call(
        second_kernel,
        f32(SLOTS * W, 2 * W),
        4,
        scratch=(pltpu.VMEM((SLOTS * W, W), jnp.float32),),
        flops=5 * 10**8,
        moved=3 * 2**20,
    )(meta, cur, got1, oth1, kept)
    return schur, lpan


def solution(mesh):
    fine = Mesh(mesh.devices.reshape(4, 4, NZ, 2), ("x", "y", "z", "core"))
    placed = (P(("x", "y"), ("z", "core")), P(), P(), P(), P())
    return jax.shard_map(
        shards,
        mesh=fine,
        in_specs=placed,
        out_specs=(P(("x", "y"), ("z", "core")), P(("x", "y"), None)),
        check_vma=False,
    )
```

```python
import jax
import jax.numpy as jnp
from jax import lax
from jax.experimental import pallas as pl
from jax.experimental.pallas import tpu as pltpu
from jax.sharding import Mesh
from jax.sharding import PartitionSpec as P

SWEEPS = 3
W = 128
H = W // 2
NP = 16
NZ = 16
SLOTS = 8
SENDS = ((8, 9), (7, 10), (6, 11), (5, 12), (4, 13), (3, 14), (2, 15), (1, 0))


def dot16(a, b):
    return jnp.dot(a, b, preferred_element_type=jnp.float32)


def split(x):
    high = x.astype(jnp.bfloat16)
    return high, (x - high.astype(jnp.float32)).astype(jnp.bfloat16)


def dot(a, b):
    left = jnp.concatenate(split(a), axis=1)
    right = jnp.concatenate(split(b), axis=1)
    both = dot16(left, jnp.concatenate([right, right], axis=0))
    n = b.shape[1]
    return both[:, :n] + both[:, n:]


def reorder(perms, k, x):
    hit = lax.broadcasted_iota(jnp.int32, (W, W), 0) == perms[k : k + 1, :]
    order = jnp.where(hit, 1.0, 0.0).astype(jnp.float32).T.astype(jnp.bfloat16)
    high, mid = split(x)
    low = (x - high.astype(jnp.float32) - mid.astype(jnp.float32)).astype(jnp.bfloat16)
    return dot16(order, high) + (dot16(order, mid) + dot16(order, low))


def index_kernel(dest, row_mask, col_mask, meta, src):
    me = lax.axis_index("x") * 4 + lax.axis_index("y")
    z = lax.axis_index("z")
    core = lax.axis_index("core")

    def invert(i, carry):
        src[0, dest[0, i]] = i
        src[1, dest[1, i]] = i
        return carry

    lax.fori_loop(0, W, invert, 0, unroll=8)

    def row_ok(k, i):
        return ((row_mask[k, i] == 1) & (i > k)).astype(jnp.int32)

    def col_ok(k, j):
        return ((col_mask[k, j] == 1) & (j > k)).astype(jnp.int32)

    head = src[0, 1]
    block = (z * 2 + core) * 2
    meta[0] = core
    meta[1] = (me == 0).astype(jnp.int32)
    meta[2] = col_ok(0, 1)
    meta[3] = row_ok(0, head)
    meta[4] = lax.shift_right_logical(head, 3)
    for k in range(2):
        for j in range(2):
            meta[64 + 2 * k + j] = col_ok(k, block + j)
    for slot in range(SLOTS):
        here = me * SLOTS + slot
        meta[8 + slot] = row_ok(0, here)
        meta[16 + slot] = row_ok(1, here)
        meta[24 + slot] = row_ok(0, src[0, here])
        meta[32 + slot] = lax.shift_right_logical(dest[1, here], 3)
        meta[40 + slot] = lax.shift_right_logical(src[1, here], 3)
        meta[56 + slot] = lax.shift_right_logical(src[0, here], 3)


def route_kernel(dest, a, own, *refs):
    got, (out, panel, last) = refs[:-3], refs[-3:]
    me = lax.axis_index("x") * 4 + lax.axis_index("y")
    root = (lax.axis_index("z") == 0) & (lax.axis_index("core") == 0)
    share = own[...] * root.astype(jnp.float32)
    for ref in got:
        share = share + ref[...]
    out[...] = jnp.zeros_like(out)
    for slot in range(SLOTS):
        left, right = share[slot, :, :W], share[slot, :, W:]
        out[lax.shift_right_logical(dest[0, me * SLOTS + slot], 3), 0] = left
        if slot < 7:
            panel[slot] = left
            panel[7 + slot] = right
        else:
            last[0] = left
            last[1] = right
        if slot < 2:
            out[:, 1 + 2 * slot] = jnp.broadcast_to(left[None], (NP, 8, W))
            out[:, 2 + 2 * slot] = jnp.broadcast_to(right[None], (NP, 8, W))
    rows = a[: 2 * W].reshape(NP, 2, 8, 2 * W)
    out[:, 5:7] = rows[..., :W]
    out[:, 7:9] = rows[..., W:]


def pack_kernel(meta, passed, last, got, out, chunk):
    chunk[...] = got[0, 5:9]

    @pl.when(meta[0] == 1)
    def _():
        out[...] = passed[...]

    @pl.when(meta[0] == 0)
    def _():
        out[:2] = last[...]
        for slot in range(SLOTS):
            out[2 + slot] = got[meta[56 + slot], 0]
        out[10:12] = got[0, 1:3]
        out[12] = got[meta[4], 3]
        out[13] = got[0, 4]


def refine(pivot):
    row = lax.broadcasted_iota(jnp.int32, (W, W), 0)
    col = lax.broadcasted_iota(jnp.int32, (W, W), 1)
    two = jnp.where(row == col, 2.0, 0.0).astype(jnp.float32)
    scale = W * (jnp.mean(pivot * pivot) + 1e-6)
    approx = pivot.T / scale
    for _ in range(SWEEPS):
        approx = dot(approx, two - dot(pivot, approx))
    return approx


def factor(meta, head, panel, chunk, perms, lpan, plow, send, lsrc):
    def tile(ref, t):
        return ref[:, t].reshape(W, W)

    def flag(i):
        return meta[i].astype(jnp.float32)

    def flagged(block, base):
        return jnp.concatenate(
            [block[s * W : (s + 1) * W] * flag(base + s) for s in range(SLOTS)], axis=0
        )

    inv0 = refine(reorder(perms, 0, tile(head, 10)))
    kept01 = reorder(perms, 0, tile(head, 11)) * flag(2)
    low_src = dot(tile(head, 12), inv0) * flag(3)
    lsrc[...] = low_src
    inv1 = refine(reorder(perms, 1, tile(head, 13) - dot(low_src, kept01)))
    col0 = jnp.concatenate([tile(panel, s) for s in range(7)] + [tile(head, 0)], axis=0)
    lpan[:, :W] = flagged(dot(col0, inv0), 8)
    ext0 = jnp.concatenate([tile(head, 2 + s) for s in range(SLOTS)], axis=0)
    ext0 = flagged(dot(ext0, inv0), 24)
    plow[...] = ext0
    col1 = jnp.concatenate([tile(panel, 7 + s) for s in range(7)] + [tile(head, 1)], axis=0)
    lpan[:, W:] = flagged(dot(col1 - dot(ext0, kept01), inv1), 16)
    for slot in range(SLOTS):
        half = pl.ds(pl.multiple_of(slot * W + meta[0] * H, H), H)
        send[meta[32 + slot], :H] = lpan[half, W:]
    send[:, H:] = jnp.broadcast_to(chunk[...].reshape(1, 32, W), (NP, 32, W))


def factor_kernel(meta, own, oth, *refs):
    @pl.when(meta[0] == 0)
    def _():
        factor(meta, own, oth, *refs)

    @pl.when(meta[0] == 1)
    def _():
        factor(meta, oth, own, *refs)


def first_kernel(meta, a, got, plow, lsrc, perms, cur, kept):
    def masked(block, k):
        return jnp.concatenate(
            [block[:, j * W : (j + 1) * W] * meta[64 + 2 * k + j].astype(jnp.float32) for j in range(2)],
            axis=1,
        )

    rows = jnp.concatenate(
        [got[:, H : H + 16].reshape(2 * W, W), got[:, H + 16 :].reshape(2 * W, W)], axis=1
    )
    up0 = reorder(perms, 0, rows[:W])
    kept0 = masked(up0, 0)
    up1 = reorder(perms, 1, rows[W:] - dot(lsrc[...], kept0))
    kept[...] = masked(up1, 1)
    prod = dot(plow[...], kept0)
    cur[...] = a[...] - prod

    @pl.when(meta[1] == 1)
    def _():
        cur[:W] = up0 - prod[:W]
        cur[W : 2 * W] = up1


def second_kernel(meta, cur, own, oth, kept, out, low):
    core = meta[0]
    for slot in range(SLOTS):
        dev = meta[40 + slot]
        low[pl.ds(pl.multiple_of(slot * W + core * H, H), H), :] = own[dev, :H]
        low[pl.ds(pl.multiple_of(slot * W + (1 - core) * H, H), H), :] = oth[dev]
    out[...] = cur[...] - dot(low[...], kept[...])


def f32(*shape):
    return jax.ShapeDtypeStruct(shape, jnp.float32)


def call(kernel, out_shape, n_in, scratch=(), flops=0, moved=0):
    smem = pl.BlockSpec(memory_space=pltpu.SMEM)
    vmem = pl.BlockSpec(memory_space=pltpu.VMEM)
    multi = isinstance(out_shape, (tuple, list))
    return pl.pallas_call(
        kernel,
        out_shape=out_shape,
        in_specs=[smem] + [vmem] * n_in,
        out_specs=[vmem] * len(out_shape) if multi else vmem,
        scratch_shapes=list(scratch),
        compiler_params=pltpu.CompilerParams(vmem_limit_bytes=24 * 2**20),
        cost_estimate=pl.CostEstimate(flops=flops, bytes_accessed=moved, transcendentals=0),
    )


def shards(a, row_perms, dest_rows, row_mask, col_mask):
    core = lax.axis_index("core")
    smem = pl.BlockSpec(memory_space=pltpu.SMEM)
    over = lax.ppermute(a, ("z", "core"), [(0, 1)]).reshape(SLOTS, NZ, 8, 2 * W)
    cut = a.reshape(SLOTS, NZ, 8, 2 * W)
    got = []
    for z0, z1 in reversed(SENDS):
        pairs, piece = [(0, 2 * z0)], cut[:, z0]
        if z1:
            pairs.append((1, 2 * z1))
            piece = jnp.where(core == 0, piece, over[:, z1])
        got.append(lax.ppermute(piece, ("z", "core"), pairs))

    out0, panel, last = call(
        route_kernel, (f32(NP, 9, 8, W), f32(14, 8, W), f32(2, 8, W)), 10, moved=2**20
    )(dest_rows, a[: 2 * W], cut[:, 0], *got)
    out0, maps = lax.optimization_barrier((out0, (dest_rows, row_mask, col_mask)))
    passed = lax.ppermute(panel, "core", [(0, 1)])
    meta = pl.pallas_call(
        index_kernel,
        out_shape=jax.ShapeDtypeStruct((W,), jnp.int32),
        in_specs=[smem] * 3,
        out_specs=smem,
        scratch_shapes=[pltpu.SMEM((2, W), jnp.int32)],
    )(*maps)
    got0 = lax.all_to_all(out0, ("x", "y"), 0, 0, tiled=True)
    payload, chunk = call(pack_kernel, (f32(14, 8, W), f32(4, 8, W)), 3, moved=2**19)(
        meta, passed, last, got0
    )

    own = lax.all_gather(payload, "z", axis=0, tiled=False)
    oth = lax.ppermute(own, "core", [(0, 1), (1, 0)])

    lpan, plow, send, lsrc = call(
        factor_kernel,
        (f32(SLOTS * W, 2 * W), f32(SLOTS * W, W), f32(NP, H + 32, W), f32(W, W)),
        4,
        flops=5 * 10**8,
        moved=4 * 2**20,
    )(meta, own, oth, chunk, row_perms)

    got1 = lax.all_to_all(send, ("x", "y"), 0, 0, tiled=True)
    oth1 = lax.ppermute(got1[:, :H], "core", [(0, 1), (1, 0)])
    cur, kept = call(
        first_kernel, (f32(SLOTS * W, 2 * W), f32(W, 2 * W)), 5, flops=5 * 10**8, moved=3 * 2**20
    )(meta, a, got1, plow, lsrc, row_perms)
    schur = call(
        second_kernel,
        f32(SLOTS * W, 2 * W),
        4,
        scratch=(pltpu.VMEM((SLOTS * W, W), jnp.float32),),
        flops=5 * 10**8,
        moved=3 * 2**20,
    )(meta, cur, got1, oth1, kept)
    return schur, lpan


def solution(mesh):
    fine = Mesh(mesh.devices.reshape(4, 4, NZ, 2), ("x", "y", "z", "core"))
    placed = (P(("x", "y"), ("z", "core")), P(), P(), P(), P())
    return jax.shard_map(
        shards,
        mesh=fine,
        in_specs=placed,
        out_specs=(P(("x", "y"), ("z", "core")), P(("x", "y"), None)),
        check_vma=False,
    )
```

```python
import jax
import jax.numpy as jnp
from jax import lax
from jax.experimental import pallas as pl
from jax.experimental.pallas import tpu as pltpu
from jax.sharding import Mesh
from jax.sharding import PartitionSpec as P

SWEEPS = 3
W = 128
H = W // 2
NP = 16
NZ = 16
SLOTS = 8


def dot16(a, b):
    return jnp.dot(a, b, preferred_element_type=jnp.float32)


def split(x):
    high = x.astype(jnp.bfloat16)
    return high, (x - high.astype(jnp.float32)).astype(jnp.bfloat16)


def dot(a, b):
    left = jnp.concatenate(split(a), axis=1)
    right = jnp.concatenate(split(b), axis=1)
    both = dot16(left, jnp.concatenate([right, right], axis=0))
    n = b.shape[1]
    return both[:, :n] + both[:, n:]


def reorder(perms, k, x):
    hit = lax.broadcasted_iota(jnp.int32, (W, W), 0) == perms[k : k + 1, :]
    order = jnp.where(hit, 1.0, 0.0).astype(jnp.float32).T.astype(jnp.bfloat16)
    high, mid = split(x)
    low = (x - high.astype(jnp.float32) - mid.astype(jnp.float32)).astype(jnp.bfloat16)
    return dot16(order, high) + (dot16(order, mid) + dot16(order, low))


def index_kernel(dest, row_mask, col_mask, meta, src):
    me = lax.axis_index("x") * 4 + lax.axis_index("y")
    z = lax.axis_index("z")
    core = lax.axis_index("core")

    def invert(i, carry):
        src[0, dest[0, i]] = i
        src[1, dest[1, i]] = i
        return carry

    lax.fori_loop(0, W, invert, 0, unroll=8)

    def row_ok(k, i):
        return ((row_mask[k, i] == 1) & (i > k)).astype(jnp.int32)

    def col_ok(k, j):
        return ((col_mask[k, j] == 1) & (j > k)).astype(jnp.int32)

    head = src[0, 1]
    block = (z * 2 + core) * 2
    meta[0] = core
    meta[1] = (me == 0).astype(jnp.int32)
    meta[2] = col_ok(0, 1)
    meta[3] = row_ok(0, head)
    meta[4] = lax.shift_right_logical(head, 3)
    for k in range(2):
        for j in range(2):
            meta[64 + 2 * k + j] = col_ok(k, block + j)
    for slot in range(SLOTS):
        here = me * SLOTS + slot
        meta[8 + slot] = row_ok(0, here)
        meta[16 + slot] = row_ok(1, here)
        meta[24 + slot] = row_ok(0, src[0, here])
        meta[32 + slot] = lax.shift_right_logical(dest[1, here], 3)
        meta[40 + slot] = lax.shift_right_logical(src[1, here], 3)
        meta[56 + slot] = lax.shift_right_logical(src[0, here], 3)


def route_kernel(dest, a, own, *refs):
    got, (out, panel, last) = refs[:-3], refs[-3:]
    me = lax.axis_index("x") * 4 + lax.axis_index("y")
    root = (lax.axis_index("z") == 0) & (lax.axis_index("core") == 0)
    share = own[...] * root.astype(jnp.float32)
    for ref in got:
        share = share + ref[...]
    out[...] = jnp.zeros_like(out)
    for slot in range(SLOTS):
        left, right = share[slot, :, :W], share[slot, :, W:]
        out[lax.shift_right_logical(dest[0, me * SLOTS + slot], 3), 0] = left
        if slot < 7:
            panel[slot] = left
            panel[7 + slot] = right
        else:
            last[0] = left
            last[1] = right
        if slot < 2:
            out[:, 1 + 2 * slot] = jnp.broadcast_to(left[None], (NP, 8, W))
            out[:, 2 + 2 * slot] = jnp.broadcast_to(right[None], (NP, 8, W))
    rows = a[: 2 * W].reshape(NP, 2, 8, 2 * W)
    out[:, 5:7] = rows[..., :W]
    out[:, 7:9] = rows[..., W:]


def pack_kernel(meta, passed, last, got, out, chunk):
    chunk[...] = got[0, 5:9]

    @pl.when(meta[0] == 1)
    def _():
        out[...] = passed[...]

    @pl.when(meta[0] == 0)
    def _():
        out[:2] = last[...]
        for slot in range(SLOTS):
            out[2 + slot] = got[meta[56 + slot], 0]
        out[10:12] = got[0, 1:3]
        out[12] = got[meta[4], 3]
        out[13] = got[0, 4]


def refine(pivot):
    row = lax.broadcasted_iota(jnp.int32, (W, W), 0)
    col = lax.broadcasted_iota(jnp.int32, (W, W), 1)
    two = jnp.where(row == col, 2.0, 0.0).astype(jnp.float32)
    scale = W * (jnp.mean(pivot * pivot) + 1e-6)
    approx = pivot.T / scale
    for _ in range(SWEEPS):
        approx = dot(approx, two - dot(pivot, approx))
    return approx


def factor(meta, head, panel, chunk, perms, lpan, plow, send, lsrc):
    def tile(ref, t):
        return ref[:, t].reshape(W, W)

    def flag(i):
        return meta[i].astype(jnp.float32)

    def flagged(block, base):
        return jnp.concatenate(
            [block[s * W : (s + 1) * W] * flag(base + s) for s in range(SLOTS)], axis=0
        )

    inv0 = refine(reorder(perms, 0, tile(head, 10)))
    kept01 = reorder(perms, 0, tile(head, 11)) * flag(2)
    low_src = dot(tile(head, 12), inv0) * flag(3)
    lsrc[...] = low_src
    inv1 = refine(reorder(perms, 1, tile(head, 13) - dot(low_src, kept01)))
    col0 = jnp.concatenate([tile(panel, s) for s in range(7)] + [tile(head, 0)], axis=0)
    lpan[:, :W] = flagged(dot(col0, inv0), 8)
    ext0 = jnp.concatenate([tile(head, 2 + s) for s in range(SLOTS)], axis=0)
    ext0 = flagged(dot(ext0, inv0), 24)
    plow[...] = ext0
    col1 = jnp.concatenate([tile(panel, 7 + s) for s in range(7)] + [tile(head, 1)], axis=0)
    lpan[:, W:] = flagged(dot(col1 - dot(ext0, kept01), inv1), 16)
    for slot in range(SLOTS):
        half = pl.ds(pl.multiple_of(slot * W + meta[0] * H, H), H)
        send[meta[32 + slot], :H] = lpan[half, W:]
    send[:, H:] = jnp.broadcast_to(chunk[...].reshape(1, 32, W), (NP, 32, W))


def factor_kernel(meta, own, oth, *refs):
    @pl.when(meta[0] == 0)
    def _():
        factor(meta, own, oth, *refs)

    @pl.when(meta[0] == 1)
    def _():
        factor(meta, oth, own, *refs)


def first_kernel(meta, a, got, plow, lsrc, perms, cur, kept):
    def masked(block, k):
        return jnp.concatenate(
            [block[:, j * W : (j + 1) * W] * meta[64 + 2 * k + j].astype(jnp.float32) for j in range(2)],
            axis=1,
        )

    rows = jnp.concatenate(
        [got[:, H : H + 16].reshape(2 * W, W), got[:, H + 16 :].reshape(2 * W, W)], axis=1
    )
    up0 = reorder(perms, 0, rows[:W])
    kept0 = masked(up0, 0)
    up1 = reorder(perms, 1, rows[W:] - dot(lsrc[...], kept0))
    kept[...] = masked(up1, 1)
    prod = dot(plow[...], kept0)
    cur[...] = a[...] - prod

    @pl.when(meta[1] == 1)
    def _():
        cur[:W] = up0 - prod[:W]
        cur[W : 2 * W] = up1


def second_kernel(meta, cur, own, oth, kept, out, low):
    core = meta[0]
    for slot in range(SLOTS):
        dev = meta[40 + slot]
        low[pl.ds(pl.multiple_of(slot * W + core * H, H), H), :] = own[dev, :H]
        low[pl.ds(pl.multiple_of(slot * W + (1 - core) * H, H), H), :] = oth[dev]
    out[...] = cur[...] - dot(low[...], kept[...])


def f32(*shape):
    return jax.ShapeDtypeStruct(shape, jnp.float32)


def call(kernel, out_shape, n_in, scratch=(), flops=0, moved=0):
    smem = pl.BlockSpec(memory_space=pltpu.SMEM)
    vmem = pl.BlockSpec(memory_space=pltpu.VMEM)
    multi = isinstance(out_shape, (tuple, list))
    return pl.pallas_call(
        kernel,
        out_shape=out_shape,
        in_specs=[smem] + [vmem] * n_in,
        out_specs=[vmem] * len(out_shape) if multi else vmem,
        scratch_shapes=list(scratch),
        compiler_params=pltpu.CompilerParams(vmem_limit_bytes=24 * 2**20),
        cost_estimate=pl.CostEstimate(flops=flops, bytes_accessed=moved, transcendentals=0),
    )


def shards(a, row_perms, dest_rows, row_mask, col_mask):
    z = lax.axis_index("z")
    smem = pl.BlockSpec(memory_space=pltpu.SMEM)
    cut = a.reshape(SLOTS, NZ, 8, 2 * W)

    def along(x, *pairs):
        return lax.ppermute(x, ("z", "core"), [(2 * src, 2 * dst) for src, dst in pairs])

    near = [along(cut[:, k], (0, k)) for k in (3, 2, 1)]
    four = along(cut[:, 4:10].transpose(1, 0, 2, 3), (0, 4))
    part, near, four = lax.optimization_barrier((cut[:, 10:13].transpose(1, 0, 2, 3), near, four))
    twelve = along(part, (0, 12))

    def held(k, up, down):
        return jnp.where(z == 4, four[up - 4], jnp.where(z == 12, twelve[down - 10], cut[:, k]))

    got = [
        *near,
        along(held(5, 6, 10), (0, 5), (4, 6)),
        along(held(13, 7, 10), (0, 13), (4, 7)),
        along(held(14, 9, 10), (0, 14), (4, 9), (12, 10)),
        along(held(15, 8, 11), (0, 15), (4, 8), (12, 11)),
        four[0],
        twelve[2],
    ]

    out0, panel, last = call(
        route_kernel, (f32(NP, 9, 8, W), f32(14, 8, W), f32(2, 8, W)), 11, moved=2**20
    )(dest_rows, a[: 2 * W], cut[:, 0], *got)
    out0, maps = lax.optimization_barrier((out0, (dest_rows, row_mask, col_mask)))
    passed = lax.ppermute(panel, "core", [(0, 1)])
    meta = pl.pallas_call(
        index_kernel,
        out_shape=jax.ShapeDtypeStruct((W,), jnp.int32),
        in_specs=[smem] * 3,
        out_specs=smem,
        scratch_shapes=[pltpu.SMEM((2, W), jnp.int32)],
    )(*maps)
    got0 = lax.all_to_all(out0, ("x", "y"), 0, 0, tiled=True)
    payload, chunk = call(pack_kernel, (f32(14, 8, W), f32(4, 8, W)), 3, moved=2**19)(
        meta, passed, last, got0
    )

    own = lax.all_gather(payload, "z", axis=0, tiled=False)
    oth = lax.ppermute(own, "core", [(0, 1), (1, 0)])

    lpan, plow, send, lsrc = call(
        factor_kernel,
        (f32(SLOTS * W, 2 * W), f32(SLOTS * W, W), f32(NP, H + 32, W), f32(W, W)),
        4,
        flops=5 * 10**8,
        moved=4 * 2**20,
    )(meta, own, oth, chunk, row_perms)

    got1 = lax.all_to_all(send, ("x", "y"), 0, 0, tiled=True)
    oth1 = lax.ppermute(got1[:, :H], "core", [(0, 1), (1, 0)])
    cur, kept = call(
        first_kernel, (f32(SLOTS * W, 2 * W), f32(W, 2 * W)), 5, flops=5 * 10**8, moved=3 * 2**20
    )(meta, a, got1, plow, lsrc, row_perms)
    schur = call(
        second_kernel,
        f32(SLOTS * W, 2 * W),
        4,
        scratch=(pltpu.VMEM((SLOTS * W, W), jnp.float32),),
        flops=5 * 10**8,
        moved=3 * 2**20,
    )(meta, cur, got1, oth1, kept)
    return schur, lpan


def solution(mesh):
    fine = Mesh(mesh.devices.reshape(4, 4, NZ, 2), ("x", "y", "z", "core"))
    placed = (P(("x", "y"), ("z", "core")), P(), P(), P(), P())
    return jax.shard_map(
        shards,
        mesh=fine,
        in_specs=placed,
        out_specs=(P(("x", "y"), ("z", "core")), P(("x", "y"), None)),
        check_vma=False,
    )
```

```python
import jax
import jax.numpy as jnp
from jax import lax
from jax.experimental import pallas as pl
from jax.experimental.pallas import tpu as pltpu
from jax.sharding import Mesh
from jax.sharding import PartitionSpec as P

SWEEPS = 3
W = 128
H = W // 2
NP = 16
NZ = 16
SLOTS = 8


def dot16(a, b):
    return jnp.dot(a, b, preferred_element_type=jnp.float32)


def split(x):
    high = x.astype(jnp.bfloat16)
    return high, (x - high.astype(jnp.float32)).astype(jnp.bfloat16)


def dot(a, b):
    left = jnp.concatenate(split(a), axis=1)
    right = jnp.concatenate(split(b), axis=1)
    both = dot16(left, jnp.concatenate([right, right], axis=0))
    n = b.shape[1]
    return both[:, :n] + both[:, n:]


def exact(x):
    high, mid = split(x)
    return high, mid, (x - high.astype(jnp.float32) - mid.astype(jnp.float32)).astype(jnp.bfloat16)


def order(perms, k):
    hit = lax.broadcasted_iota(jnp.int32, (W, W), 0) == perms[k : k + 1, :]
    return jnp.where(hit, 1.0, 0.0).astype(jnp.float32)


def reorder_rows(perms, k, x):
    move = order(perms, k).T.astype(jnp.bfloat16)
    high, mid, low = exact(x)
    return dot16(move, high) + (dot16(move, mid) + dot16(move, low))


def reorder_columns(perms, k, x):
    move = order(perms, k).astype(jnp.bfloat16)
    high, mid, low = exact(x)
    return dot16(high, move) + (dot16(mid, move) + dot16(low, move))


def index_kernel(dest, row_mask, col_mask, meta, src):
    me = lax.axis_index("x") * 4 + lax.axis_index("y")
    z = lax.axis_index("z")
    core = lax.axis_index("core")

    def invert(i, carry):
        src[0, dest[0, i]] = i
        src[1, dest[1, i]] = i
        return carry

    lax.fori_loop(0, W, invert, 0, unroll=8)

    def row_ok(k, i):
        return ((row_mask[k, i] == 1) & (i > k)).astype(jnp.int32)

    def col_ok(k, j):
        return ((col_mask[k, j] == 1) & (j > k)).astype(jnp.int32)

    head = src[0, 1]
    block = (z * 2 + core) * 2
    meta[0] = core
    meta[1] = (me == 0).astype(jnp.int32)
    meta[2] = col_ok(0, 1)
    meta[3] = row_ok(0, head)
    meta[4] = lax.shift_right_logical(head, 3)
    for k in range(2):
        for j in range(2):
            meta[64 + 2 * k + j] = col_ok(k, block + j)
    for slot in range(SLOTS):
        here = me * SLOTS + slot
        meta[8 + slot] = row_ok(0, here)
        meta[16 + slot] = row_ok(1, here)
        meta[24 + slot] = row_ok(0, src[0, here])
        meta[32 + slot] = lax.shift_right_logical(dest[1, here], 3)
        meta[40 + slot] = lax.shift_right_logical(src[1, here], 3)
        meta[56 + slot] = lax.shift_right_logical(src[0, here], 3)


def route_kernel(dest, a, own, *refs):
    got, (out, panel, last) = refs[:-3], refs[-3:]
    me = lax.axis_index("x") * 4 + lax.axis_index("y")
    root = (lax.axis_index("z") == 0) & (lax.axis_index("core") == 0)
    share = own[...] * root.astype(jnp.float32)
    for ref in got:
        share = share + ref[...]
    for slot in range(SLOTS):
        left, right = share[slot, :, :W], share[slot, :, W:]
        out[lax.shift_right_logical(dest[0, me * SLOTS + slot], 3), 0] = left
        if slot < 7:
            panel[slot] = left
            panel[7 + slot] = right
        else:
            last[0] = left
            last[1] = right
        if slot < 2:
            out[:, 1 + 2 * slot] = jnp.broadcast_to(left[None], (NP, 8, W))
            out[:, 2 + 2 * slot] = jnp.broadcast_to(right[None], (NP, 8, W))
    rows = a[: 2 * W].reshape(NP, 2, 8, 2 * W)
    out[:, 5:7] = rows[..., :W]
    out[:, 7:9] = rows[..., W:]


def pack_kernel(meta, passed, last, got, out, chunk):
    chunk[...] = got[0, 5:9]

    @pl.when(meta[0] == 1)
    def _():
        out[...] = passed[...]

    @pl.when(meta[0] == 0)
    def _():
        out[:2] = last[...]
        for slot in range(SLOTS):
            out[2 + slot] = got[meta[56 + slot], 0]
        out[10:12] = got[0, 1:3]
        out[12] = got[meta[4], 3]
        out[13] = got[0, 4]


def refine(block):
    row = lax.broadcasted_iota(jnp.int32, (W, W), 0)
    col = lax.broadcasted_iota(jnp.int32, (W, W), 1)
    one = jnp.where(row == col, 1.0, 0.0).astype(jnp.float32)
    scale = W * (jnp.mean(block * block) + 1e-6)
    approx = block.T / scale
    rest = one - dot(block, approx)
    for sweep in range(SWEEPS):
        approx = approx + dot(approx, rest)
        if sweep + 1 < SWEEPS:
            rest = dot(rest, rest)
    return approx


def tile(ref, t):
    return ref[:, t].reshape(W, W)


def flagged(meta, block, base):
    return jnp.concatenate(
        [block[s * W : (s + 1) * W] * meta[base + s].astype(jnp.float32) for s in range(SLOTS)], axis=0
    )


def factor(meta, head, panel, send, plow, low1, inv0, lsrc):
    inv = refine(tile(head, 10))
    inv0[...] = inv
    kept01 = tile(head, 11) * meta[2].astype(jnp.float32)
    low_src = dot(tile(head, 12), inv) * meta[3].astype(jnp.float32)
    lsrc[...] = low_src
    inv1 = refine(tile(head, 13) - dot(low_src, kept01))
    ext0 = jnp.concatenate([tile(head, 2 + s) for s in range(SLOTS)], axis=0)
    ext0 = flagged(meta, dot(ext0, inv), 24)
    plow[...] = ext0
    col1 = jnp.concatenate([tile(panel, 7 + s) for s in range(7)] + [tile(head, 1)], axis=0)
    low1[...] = flagged(meta, dot(col1 - dot(ext0, kept01), inv1), 16)
    for slot in range(SLOTS):
        half = pl.ds(pl.multiple_of(slot * W + meta[0] * H, H), H)
        send[meta[32 + slot], :H] = low1[half, :]


def factor_kernel(meta, own, oth, chunk, send, *refs):
    @pl.when(meta[0] == 0)
    def _():
        factor(meta, own, oth, send, *refs)

    @pl.when(meta[0] == 1)
    def _():
        factor(meta, oth, own, send, *refs)

    send[:, H:] = jnp.broadcast_to(chunk[...].reshape(1, 32, W), (NP, 32, W))


def panels_kernel(meta, own, oth, low1, inv0, perms, lpan):
    def write(head, panel):
        col0 = jnp.concatenate([tile(panel, s) for s in range(7)] + [tile(head, 0)], axis=0)
        lpan[:, :W] = flagged(meta, dot(col0, reorder_columns(perms, 0, inv0[...])), 8)

    @pl.when(meta[0] == 0)
    def _():
        write(own, oth)

    @pl.when(meta[0] == 1)
    def _():
        write(oth, own)

    lpan[:, W:] = reorder_columns(perms, 1, low1[...])


def first_kernel(meta, a, got, plow, lsrc, perms, cur, kept):
    def masked(block, k):
        return jnp.concatenate(
            [block[:, j * W : (j + 1) * W] * meta[64 + 2 * k + j].astype(jnp.float32) for j in range(2)],
            axis=1,
        )

    rows = jnp.concatenate(
        [got[:, H : H + 16].reshape(2 * W, W), got[:, H + 16 :].reshape(2 * W, W)], axis=1
    )
    kept0 = masked(rows[:W], 0)
    next1 = rows[W:] - dot(lsrc[...], kept0)
    kept[...] = masked(next1, 1)
    prod = dot(plow[...], kept0)
    cur[...] = a[...] - prod

    @pl.when(meta[1] == 1)
    def _():
        cur[:W] = reorder_rows(perms, 0, rows[:W]) - prod[:W]
        cur[W : 2 * W] = reorder_rows(perms, 1, next1)


def second_kernel(meta, cur, own, oth, kept, out, low):
    core = meta[0]
    for slot in range(SLOTS):
        dev = meta[40 + slot]
        low[pl.ds(pl.multiple_of(slot * W + core * H, H), H), :] = own[dev, :H]
        low[pl.ds(pl.multiple_of(slot * W + (1 - core) * H, H), H), :] = oth[dev]
    out[...] = cur[...] - dot(low[...], kept[...])


def f32(*shape):
    return jax.ShapeDtypeStruct(shape, jnp.float32)


def call(kernel, out_shape, n_in, scratch=(), flops=0, moved=0):
    smem = pl.BlockSpec(memory_space=pltpu.SMEM)
    vmem = pl.BlockSpec(memory_space=pltpu.VMEM)
    multi = isinstance(out_shape, (tuple, list))
    return pl.pallas_call(
        kernel,
        out_shape=out_shape,
        in_specs=[smem] + [vmem] * n_in,
        out_specs=[vmem] * len(out_shape) if multi else vmem,
        scratch_shapes=list(scratch),
        compiler_params=pltpu.CompilerParams(vmem_limit_bytes=24 * 2**20),
        cost_estimate=pl.CostEstimate(flops=flops, bytes_accessed=moved, transcendentals=0),
    )


def shards(a, row_perms, dest_rows, row_mask, col_mask):
    core = lax.axis_index("core")
    smem = pl.BlockSpec(memory_space=pltpu.SMEM)
    cut = a.reshape(SLOTS, NZ, 8, 2 * W)
    over = lax.ppermute(cut[:, 8:].transpose(1, 0, 2, 3), ("z", "core"), [(0, 1)])
    pieces = [jnp.where(core == 0, cut[:, step % 8], over[8 - step]) for step in range(1, 9)]
    pieces = lax.optimization_barrier(pieces)
    got = []
    for step in range(1, 9):
        pairs = [(1, 2 * (NZ - step))]
        if step < 8:
            pairs.append((0, 2 * step))
        got.append(lax.ppermute(pieces[step - 1], ("z", "core"), pairs))

    out0, panel, last = call(
        route_kernel, (f32(NP, 9, 8, W), f32(14, 8, W), f32(2, 8, W)), 10, moved=2**20
    )(dest_rows, a[: 2 * W], pieces[7], *got)
    out0, maps = lax.optimization_barrier((out0, (dest_rows, row_mask, col_mask)))
    passed = lax.ppermute(panel, "core", [(0, 1)])
    meta = pl.pallas_call(
        index_kernel,
        out_shape=jax.ShapeDtypeStruct((W,), jnp.int32),
        in_specs=[smem] * 3,
        out_specs=smem,
        scratch_shapes=[pltpu.SMEM((2, W), jnp.int32)],
    )(*maps)
    got0 = lax.all_to_all(out0, ("x", "y"), 0, 0, tiled=True)
    payload, chunk = call(pack_kernel, (f32(14, 8, W), f32(4, 8, W)), 3, moved=2**19)(
        meta, passed, last, got0
    )

    own = lax.all_gather(payload, "z", axis=0, tiled=False)
    oth = lax.ppermute(own, "core", [(0, 1), (1, 0)])

    send, plow, low1, inv0, lsrc = call(
        factor_kernel,
        (f32(NP, H + 32, W), f32(SLOTS * W, W), f32(SLOTS * W, W), f32(W, W), f32(W, W)),
        3,
        flops=5 * 10**8,
        moved=4 * 2**20,
    )(meta, own, oth, chunk)

    got1 = lax.all_to_all(send, ("x", "y"), 0, 0, tiled=True)
    lpan = call(panels_kernel, f32(SLOTS * W, 2 * W), 5, flops=5 * 10**8, moved=4 * 2**20)(
        meta, own, oth, low1, inv0, row_perms
    )
    got1, lpan = lax.optimization_barrier((got1, lpan))
    oth1 = lax.ppermute(got1[:, :H], "core", [(0, 1), (1, 0)])
    cur, kept = call(
        first_kernel, (f32(SLOTS * W, 2 * W), f32(W, 2 * W)), 5, flops=5 * 10**8, moved=3 * 2**20
    )(meta, a, got1, plow, lsrc, row_perms)
    schur = call(
        second_kernel,
        f32(SLOTS * W, 2 * W),
        4,
        scratch=(pltpu.VMEM((SLOTS * W, W), jnp.float32),),
        flops=5 * 10**8,
        moved=3 * 2**20,
    )(meta, cur, got1, oth1, kept)
    return schur, lpan


def solution(mesh):
    fine = Mesh(mesh.devices.reshape(4, 4, NZ, 2), ("x", "y", "z", "core"))
    placed = (P(("x", "y"), ("z", "core")), P(), P(), P(), P())
    return jax.shard_map(
        shards,
        mesh=fine,
        in_specs=placed,
        out_specs=(P(("x", "y"), ("z", "core")), P(("x", "y"), None)),
        check_vma=False,
    )
```

```python
import jax
import jax.numpy as jnp
from jax import lax
from jax.experimental import pallas as pl
from jax.experimental.pallas import tpu as pltpu
from jax.sharding import Mesh
from jax.sharding import PartitionSpec as P

SWEEPS = 3
W = 128
H = W // 2
NP = 16
NZ = 16
SLOTS = 8
SENDS = ((1, 15), (2, 14), (3, 13), (4, 12), (5, 11), (6, 10), (7, 8), (9, 0))


def dot16(a, b):
    return jnp.dot(a, b, preferred_element_type=jnp.float32)


def split(x):
    high = x.astype(jnp.bfloat16)
    return high, (x - high.astype(jnp.float32)).astype(jnp.bfloat16)


def dot(a, b):
    left = jnp.concatenate(split(a), axis=1)
    right = jnp.concatenate(split(b), axis=1)
    both = dot16(left, jnp.concatenate([right, right], axis=0))
    n = b.shape[1]
    return both[:, :n] + both[:, n:]


def exact(x):
    high, mid = split(x)
    return high, mid, (x - high.astype(jnp.float32) - mid.astype(jnp.float32)).astype(jnp.bfloat16)


def order(perms, k):
    hit = lax.broadcasted_iota(jnp.int32, (W, W), 0) == perms[k : k + 1, :]
    return jnp.where(hit, 1.0, 0.0).astype(jnp.float32)


def reorder_rows(perms, k, x):
    move = order(perms, k).T.astype(jnp.bfloat16)
    high, mid, low = exact(x)
    return dot16(move, high) + (dot16(move, mid) + dot16(move, low))


def reorder_columns(perms, k, x):
    move = order(perms, k).astype(jnp.bfloat16)
    high, mid, low = exact(x)
    return dot16(high, move) + (dot16(mid, move) + dot16(low, move))


def index_kernel(dest, row_mask, col_mask, meta, src):
    me = lax.axis_index("x") * 4 + lax.axis_index("y")
    z = lax.axis_index("z")
    core = lax.axis_index("core")

    def invert(i, carry):
        src[0, dest[0, i]] = i
        src[1, dest[1, i]] = i
        return carry

    lax.fori_loop(0, W, invert, 0, unroll=8)

    def row_ok(k, i):
        return ((row_mask[k, i] == 1) & (i > k)).astype(jnp.int32)

    def col_ok(k, j):
        return ((col_mask[k, j] == 1) & (j > k)).astype(jnp.int32)

    head = src[0, 1]
    block = (z * 2 + core) * 2
    meta[0] = core
    meta[1] = (me == 0).astype(jnp.int32)
    meta[2] = col_ok(0, 1)
    meta[3] = row_ok(0, head)
    meta[4] = lax.shift_right_logical(head, 3)
    for k in range(2):
        for j in range(2):
            meta[64 + 2 * k + j] = col_ok(k, block + j)
    for slot in range(SLOTS):
        here = me * SLOTS + slot
        meta[8 + slot] = row_ok(0, here)
        meta[16 + slot] = row_ok(1, here)
        meta[24 + slot] = row_ok(0, src[0, here])
        meta[32 + slot] = lax.shift_right_logical(dest[1, here], 3)
        meta[40 + slot] = lax.shift_right_logical(src[1, here], 3)
        meta[56 + slot] = lax.shift_right_logical(src[0, here], 3)


def cut_kernel(a, over, *refs):
    outs, sem = refs[:9], refs[9]
    z, core = lax.axis_index("z"), lax.axis_index("core")

    def bring(source, places):
        copies = [
            pltpu.make_async_copy(source.at[:, place], outs[i], sem.at[i]) for i, place in places
        ]
        for copy in copies:
            copy.start()
        for copy in copies:
            copy.wait()

    @pl.when((z == 0) & (core == 0))
    def _():
        bring(a, [(i, z0) for i, (z0, _) in enumerate(SENDS)] + [(8, 0)])

    @pl.when((z == 0) & (core == 1))
    def _():
        bring(over, [(i, z1) for i, (_, z1) in enumerate(SENDS) if z1])


def route_kernel(dest, a, own, *refs):
    got, (out, panel, last) = refs[:-3], refs[-3:]
    me = lax.axis_index("x") * 4 + lax.axis_index("y")
    root = (lax.axis_index("z") == 0) & (lax.axis_index("core") == 0)
    share = jnp.where(root, own[...], 0.0)
    for ref in got:
        share = share + ref[...]
    for slot in range(SLOTS):
        left, right = share[slot, :, :W], share[slot, :, W:]
        out[lax.shift_right_logical(dest[0, me * SLOTS + slot], 3), 0] = left
        if slot < 7:
            panel[slot] = left
            panel[7 + slot] = right
        else:
            last[0] = left
            last[1] = right
        if slot < 2:
            out[:, 1 + 2 * slot] = jnp.broadcast_to(left[None], (NP, 8, W))
            out[:, 2 + 2 * slot] = jnp.broadcast_to(right[None], (NP, 8, W))
    rows = a[: 2 * W].reshape(NP, 2, 8, 2 * W)
    out[:, 5:7] = rows[..., :W]
    out[:, 7:9] = rows[..., W:]


def pack_kernel(meta, passed, last, got, out, chunk):
    chunk[...] = got[0, 5:9]

    @pl.when(meta[0] == 1)
    def _():
        out[...] = passed[...]

    @pl.when(meta[0] == 0)
    def _():
        out[:2] = last[...]
        for slot in range(SLOTS):
            out[2 + slot] = got[meta[56 + slot], 0]
        out[10:12] = got[0, 1:3]
        out[12] = got[meta[4], 3]
        out[13] = got[0, 4]


def refine(block):
    row = lax.broadcasted_iota(jnp.int32, (W, W), 0)
    col = lax.broadcasted_iota(jnp.int32, (W, W), 1)
    one = jnp.where(row == col, 1.0, 0.0).astype(jnp.float32)
    scale = W * (jnp.mean(block * block) + 1e-6)
    approx = block.T / scale
    rest = one - dot(block, approx)
    for sweep in range(SWEEPS):
        approx = approx + dot(approx, rest)
        if sweep + 1 < SWEEPS:
            rest = dot(rest, rest)
    return approx


def tile(ref, t):
    return ref[:, t].reshape(W, W)


def flagged(meta, block, base):
    return jnp.concatenate(
        [block[s * W : (s + 1) * W] * meta[base + s].astype(jnp.float32) for s in range(SLOTS)], axis=0
    )


def factor(meta, head, panel, send, plow, low1, inv0, lsrc):
    inv = refine(tile(head, 10))
    inv0[...] = inv
    kept01 = tile(head, 11) * meta[2].astype(jnp.float32)
    low_src = dot(tile(head, 12), inv) * meta[3].astype(jnp.float32)
    lsrc[...] = low_src
    inv1 = refine(tile(head, 13) - dot(low_src, kept01))
    ext0 = jnp.concatenate([tile(head, 2 + s) for s in range(SLOTS)], axis=0)
    ext0 = flagged(meta, dot(ext0, inv), 24)
    plow[...] = ext0
    col1 = jnp.concatenate([tile(panel, 7 + s) for s in range(7)] + [tile(head, 1)], axis=0)
    low1[...] = flagged(meta, dot(col1 - dot(ext0, kept01), inv1), 16)
    for slot in range(SLOTS):
        half = pl.ds(pl.multiple_of(slot * W + meta[0] * H, H), H)
        send[meta[32 + slot], :H] = low1[half, :]


def factor_kernel(meta, own, oth, chunk, send, *refs):
    @pl.when(meta[0] == 0)
    def _():
        factor(meta, own, oth, send, *refs)

    @pl.when(meta[0] == 1)
    def _():
        factor(meta, oth, own, send, *refs)

    send[:, H:] = jnp.broadcast_to(chunk[...].reshape(1, 32, W), (NP, 32, W))


def panels_kernel(meta, own, oth, low1, inv0, perms, lpan):
    def write(head, panel):
        col0 = jnp.concatenate([tile(panel, s) for s in range(7)] + [tile(head, 0)], axis=0)
        lpan[:, :W] = flagged(meta, dot(col0, reorder_columns(perms, 0, inv0[...])), 8)

    @pl.when(meta[0] == 0)
    def _():
        write(own, oth)

    @pl.when(meta[0] == 1)
    def _():
        write(oth, own)

    lpan[:, W:] = reorder_columns(perms, 1, low1[...])


def first_kernel(meta, a, got, plow, lsrc, perms, cur, kept):
    def masked(block, k):
        return jnp.concatenate(
            [block[:, j * W : (j + 1) * W] * meta[64 + 2 * k + j].astype(jnp.float32) for j in range(2)],
            axis=1,
        )

    rows = jnp.concatenate(
        [got[:, H : H + 16].reshape(2 * W, W), got[:, H + 16 :].reshape(2 * W, W)], axis=1
    )
    kept0 = masked(rows[:W], 0)
    next1 = rows[W:] - dot(lsrc[...], kept0)
    kept[...] = masked(next1, 1)
    prod = dot(plow[...], kept0)
    cur[...] = a[...] - prod

    @pl.when(meta[1] == 1)
    def _():
        cur[:W] = reorder_rows(perms, 0, rows[:W]) - prod[:W]
        cur[W : 2 * W] = reorder_rows(perms, 1, next1)


def second_kernel(meta, cur, own, oth, kept, out, low):
    core = meta[0]
    for slot in range(SLOTS):
        dev = meta[40 + slot]
        low[pl.ds(pl.multiple_of(slot * W + core * H, H), H), :] = own[dev, :H]
        low[pl.ds(pl.multiple_of(slot * W + (1 - core) * H, H), H), :] = oth[dev]
    out[...] = cur[...] - dot(low[...], kept[...])


def f32(*shape):
    return jax.ShapeDtypeStruct(shape, jnp.float32)


def call(kernel, out_shape, n_in, scratch=(), flops=0, moved=0):
    smem = pl.BlockSpec(memory_space=pltpu.SMEM)
    vmem = pl.BlockSpec(memory_space=pltpu.VMEM)
    multi = isinstance(out_shape, (tuple, list))
    return pl.pallas_call(
        kernel,
        out_shape=out_shape,
        in_specs=[smem] + [vmem] * n_in,
        out_specs=[vmem] * len(out_shape) if multi else vmem,
        scratch_shapes=list(scratch),
        compiler_params=pltpu.CompilerParams(vmem_limit_bytes=24 * 2**20),
        cost_estimate=pl.CostEstimate(flops=flops, bytes_accessed=moved, transcendentals=0),
    )


def shards(a, row_perms, dest_rows, row_mask, col_mask):
    smem = pl.BlockSpec(memory_space=pltpu.SMEM)
    cut = a.reshape(SLOTS, NZ, 8, 2 * W)
    over = lax.ppermute(a, ("z", "core"), [(0, 1)]).reshape(SLOTS, NZ, 8, 2 * W)
    block = f32(SLOTS, 8, 2 * W)
    hbm, vmem = pl.BlockSpec(memory_space=pltpu.HBM), pl.BlockSpec(memory_space=pltpu.VMEM)
    *pieces, own0 = pl.pallas_call(
        cut_kernel,
        out_shape=[block] * 9,
        in_specs=[hbm, vmem],
        out_specs=[vmem] * 9,
        scratch_shapes=[pltpu.SemaphoreType.DMA((9,))],
        compiler_params=pltpu.CompilerParams(vmem_limit_bytes=8 * 2**20),
    )(cut, over)
    got = []
    for (z0, z1), piece in zip(SENDS, pieces):
        pairs = ([(1, 2 * z1)] if z1 else []) + [(0, 2 * z0)]
        got.append(lax.ppermute(piece, ("z", "core"), pairs))

    out0, panel, last = call(
        route_kernel, (f32(NP, 9, 8, W), f32(14, 8, W), f32(2, 8, W)), 10, moved=2**20
    )(dest_rows, a[: 2 * W], own0, *got)
    out0, maps = lax.optimization_barrier((out0, (dest_rows, row_mask, col_mask)))
    passed = lax.ppermute(panel, "core", [(0, 1)])
    meta = pl.pallas_call(
        index_kernel,
        out_shape=jax.ShapeDtypeStruct((W,), jnp.int32),
        in_specs=[smem] * 3,
        out_specs=smem,
        scratch_shapes=[pltpu.SMEM((2, W), jnp.int32)],
        compiler_params=pltpu.CompilerParams(vmem_limit_bytes=8 * 2**20),
    )(*maps)
    got0 = lax.all_to_all(out0, ("x", "y"), 0, 0, tiled=True)
    payload, chunk = call(pack_kernel, (f32(14, 8, W), f32(4, 8, W)), 3, moved=2**19)(
        meta, passed, last, got0
    )

    own = lax.all_gather(payload, "z", axis=0, tiled=False)
    oth = lax.ppermute(own, "core", [(0, 1), (1, 0)])

    send, plow, low1, inv0, lsrc = call(
        factor_kernel,
        (f32(NP, H + 32, W), f32(SLOTS * W, W), f32(SLOTS * W, W), f32(W, W), f32(W, W)),
        3,
        flops=5 * 10**8,
        moved=4 * 2**20,
    )(meta, own, oth, chunk)

    got1 = lax.all_to_all(send, ("x", "y"), 0, 0, tiled=True)
    lpan = call(panels_kernel, f32(SLOTS * W, 2 * W), 5, flops=5 * 10**8, moved=4 * 2**20)(
        meta, own, oth, low1, inv0, row_perms
    )
    got1, lpan = lax.optimization_barrier((got1, lpan))
    oth1 = lax.ppermute(got1[:, :H], "core", [(0, 1), (1, 0)])
    cur, kept = call(
        first_kernel, (f32(SLOTS * W, 2 * W), f32(W, 2 * W)), 5, flops=5 * 10**8, moved=3 * 2**20
    )(meta, a, got1, plow, lsrc, row_perms)
    schur = call(
        second_kernel,
        f32(SLOTS * W, 2 * W),
        4,
        scratch=(pltpu.VMEM((SLOTS * W, W), jnp.float32),),
        flops=5 * 10**8,
        moved=3 * 2**20,
    )(meta, cur, got1, oth1, kept)
    return schur, lpan


def solution(mesh):
    fine = Mesh(mesh.devices.reshape(4, 4, NZ, 2), ("x", "y", "z", "core"))
    placed = (P(("x", "y"), ("z", "core")), P(), P(), P(), P())
    return jax.shard_map(
        shards,
        mesh=fine,
        in_specs=placed,
        out_specs=(P(("x", "y"), ("z", "core")), P(("x", "y"), None)),
        check_vma=False,
    )
```

```python
import jax
import jax.numpy as jnp
from jax import lax
from jax.experimental import pallas as pl
from jax.experimental.pallas import tpu as pltpu
from jax.sharding import Mesh
from jax.sharding import PartitionSpec as P

SWEEPS = 3
W = 128
H = W // 2
NP = 16
NZ = 16
SLOTS = 8
SENDS = ((1, 15), (2, 14), (7, 9), (8, 10), (6, 11), (5, 12), (4, 13), (3, 0))


def dot16(a, b):
    return jnp.dot(a, b, preferred_element_type=jnp.float32)


def split(x):
    high = x.astype(jnp.bfloat16)
    return high, (x - high.astype(jnp.float32)).astype(jnp.bfloat16)


def dot(a, b):
    left = jnp.concatenate(split(a), axis=1)
    right = jnp.concatenate(split(b), axis=1)
    both = dot16(left, jnp.concatenate([right, right], axis=0))
    n = b.shape[1]
    return both[:, :n] + both[:, n:]


def exact(x):
    high, mid = split(x)
    return high, mid, (x - high.astype(jnp.float32) - mid.astype(jnp.float32)).astype(jnp.bfloat16)


def order(perms, k):
    hit = lax.broadcasted_iota(jnp.int32, (W, W), 0) == perms[k : k + 1, :]
    return jnp.where(hit, 1.0, 0.0).astype(jnp.float32)


def reorder_rows(perms, k, x):
    move = order(perms, k).T.astype(jnp.bfloat16)
    high, mid, low = exact(x)
    return dot16(move, high) + (dot16(move, mid) + dot16(move, low))


def reorder_columns(perms, k, x):
    move = order(perms, k).astype(jnp.bfloat16)
    high, mid, low = exact(x)
    return dot16(high, move) + (dot16(mid, move) + dot16(low, move))


def index_kernel(dest, row_mask, col_mask, meta, src):
    me = lax.axis_index("x") * 4 + lax.axis_index("y")
    z = lax.axis_index("z")
    core = lax.axis_index("core")

    def invert(i, carry):
        src[0, dest[0, i]] = i
        src[1, dest[1, i]] = i
        return carry

    lax.fori_loop(0, W, invert, 0, unroll=8)

    def row_ok(k, i):
        return ((row_mask[k, i] == 1) & (i > k)).astype(jnp.int32)

    def col_ok(k, j):
        return ((col_mask[k, j] == 1) & (j > k)).astype(jnp.int32)

    head = src[0, 1]
    block = (z * 2 + core) * 2
    meta[0] = core
    meta[1] = (me == 0).astype(jnp.int32)
    meta[2] = col_ok(0, 1)
    meta[3] = row_ok(0, head)
    meta[4] = lax.shift_right_logical(head, 3)
    for k in range(2):
        for j in range(2):
            meta[64 + 2 * k + j] = col_ok(k, block + j)
    for slot in range(SLOTS):
        here = me * SLOTS + slot
        meta[8 + slot] = row_ok(0, here)
        meta[16 + slot] = row_ok(1, here)
        meta[24 + slot] = row_ok(0, src[0, here])
        meta[32 + slot] = lax.shift_right_logical(dest[1, here], 3)
        meta[40 + slot] = lax.shift_right_logical(src[1, here], 3)
        meta[56 + slot] = lax.shift_right_logical(src[0, here], 3)


def route_kernel(dest, a, own, *refs):
    got, (out, panel, last) = refs[:-3], refs[-3:]
    me = lax.axis_index("x") * 4 + lax.axis_index("y")
    root = (lax.axis_index("z") == 0) & (lax.axis_index("core") == 0)
    share = own[...] * root.astype(jnp.float32)
    for ref in got:
        share = share + ref[...]
    for slot in range(SLOTS):
        left, right = share[slot, :, :W], share[slot, :, W:]
        out[lax.shift_right_logical(dest[0, me * SLOTS + slot], 3), 0] = left
        if slot < 7:
            panel[slot] = left
            panel[7 + slot] = right
        else:
            last[0] = left
            last[1] = right
        if slot < 2:
            out[:, 1 + 2 * slot] = jnp.broadcast_to(left[None], (NP, 8, W))
            out[:, 2 + 2 * slot] = jnp.broadcast_to(right[None], (NP, 8, W))
    rows = a[: 2 * W].reshape(NP, 2, 8, 2 * W)
    out[:, 5:7] = rows[..., :W]
    out[:, 7:9] = rows[..., W:]


def pack_kernel(meta, passed, last, got, out, chunk):
    chunk[...] = got[0, 5:9]

    @pl.when(meta[0] == 1)
    def _():
        out[...] = passed[...]

    @pl.when(meta[0] == 0)
    def _():
        out[:2] = last[...]
        for slot in range(SLOTS):
            out[2 + slot] = got[meta[56 + slot], 0]
        out[10:12] = got[0, 1:3]
        out[12] = got[meta[4], 3]
        out[13] = got[0, 4]


def refine(block):
    row = lax.broadcasted_iota(jnp.int32, (W, W), 0)
    col = lax.broadcasted_iota(jnp.int32, (W, W), 1)
    one = jnp.where(row == col, 1.0, 0.0).astype(jnp.float32)
    scale = W * (jnp.mean(block * block) + 1e-6)
    approx = block.T / scale
    rest = one - dot(block, approx)
    for sweep in range(SWEEPS):
        approx = approx + dot(approx, rest)
        if sweep + 1 < SWEEPS:
            rest = dot(rest, rest)
    return approx


def tile(ref, t):
    return ref[:, t].reshape(W, W)


def flagged(meta, block, base):
    return jnp.concatenate(
        [block[s * W : (s + 1) * W] * meta[base + s].astype(jnp.float32) for s in range(SLOTS)], axis=0
    )


def lower1(meta, head, panel, ext0, inv1):
    kept01 = tile(head, 11) * meta[2].astype(jnp.float32)
    col1 = jnp.concatenate([tile(panel, 7 + s) for s in range(7)] + [tile(head, 1)], axis=0)
    return flagged(meta, dot(col1 - dot(ext0, kept01), inv1[...]), 16)


def factor(meta, head, panel, send, plow, inv0, inv1, lsrc, low1):
    inv = refine(tile(head, 10))
    inv0[...] = inv
    kept01 = tile(head, 11) * meta[2].astype(jnp.float32)
    low_src = dot(tile(head, 12), inv) * meta[3].astype(jnp.float32)
    lsrc[...] = low_src
    inv1[...] = refine(tile(head, 13) - dot(low_src, kept01))
    ext0 = jnp.concatenate([tile(head, 2 + s) for s in range(SLOTS)], axis=0)
    ext0 = flagged(meta, dot(ext0, inv), 24)
    plow[...] = ext0
    low1[...] = lower1(meta, head, panel, ext0, inv1)
    for slot in range(SLOTS):
        half = pl.ds(pl.multiple_of(slot * W + meta[0] * H, H), H)
        send[meta[32 + slot], :H] = low1[half, :]


def factor_kernel(meta, own, oth, chunk, send, *refs):
    @pl.when(meta[0] == 0)
    def _():
        factor(meta, own, oth, send, *refs)

    @pl.when(meta[0] == 1)
    def _():
        factor(meta, oth, own, send, *refs)

    send[:, H:] = jnp.broadcast_to(chunk[...].reshape(1, 32, W), (NP, 32, W))


def panels_kernel(meta, own, oth, plow, inv0, inv1, perms, lpan):
    def write(head, panel):
        col0 = jnp.concatenate([tile(panel, s) for s in range(7)] + [tile(head, 0)], axis=0)
        lpan[:, :W] = flagged(meta, dot(col0, reorder_columns(perms, 0, inv0[...])), 8)
        low = lower1(meta, head, panel, plow[...], inv1)
        lpan[:, W:] = reorder_columns(perms, 1, low)

    @pl.when(meta[0] == 0)
    def _():
        write(own, oth)

    @pl.when(meta[0] == 1)
    def _():
        write(oth, own)


def subtract(meta, half_of, kept, out, half):
    low = jnp.concatenate([half_of(meta[40 + slot]) for slot in range(SLOTS)], axis=0)
    prod = dot(low, kept[...])
    for slot in range(SLOTS):
        here = pl.ds(pl.multiple_of(slot * W + half * H, H), H)
        out[here, :] = out[here, :] - prod[slot * H : (slot + 1) * H]


def first_kernel(meta, a, got, plow, lsrc, perms, cur, kept):
    def masked(block, k):
        return jnp.concatenate(
            [block[:, j * W : (j + 1) * W] * meta[64 + 2 * k + j].astype(jnp.float32) for j in range(2)],
            axis=1,
        )

    rows = jnp.concatenate(
        [got[:, H : H + 16].reshape(2 * W, W), got[:, H + 16 :].reshape(2 * W, W)], axis=1
    )
    kept0 = masked(rows[:W], 0)
    next1 = rows[W:] - dot(lsrc[...], kept0)
    kept[...] = masked(next1, 1)
    prod = dot(plow[...], kept0)
    cur[...] = a[...] - prod

    @pl.when(meta[1] == 1)
    def _():
        cur[:W] = reorder_rows(perms, 0, rows[:W]) - prod[:W]
        cur[W : 2 * W] = reorder_rows(perms, 1, next1)

    subtract(meta, lambda dev: got[dev, :H], kept, cur, meta[0])


def second_kernel(meta, cur, oth, kept, out):
    out[...] = cur[...]
    subtract(meta, lambda dev: oth[dev], kept, out, 1 - meta[0])


def f32(*shape):
    return jax.ShapeDtypeStruct(shape, jnp.float32)


def call(kernel, out_shape, n_in, scratch=(), flops=0, moved=0):
    smem = pl.BlockSpec(memory_space=pltpu.SMEM)
    vmem = pl.BlockSpec(memory_space=pltpu.VMEM)
    out_specs = [vmem] * len(out_shape) if isinstance(out_shape, tuple) else vmem
    return pl.pallas_call(
        kernel,
        out_shape=out_shape,
        in_specs=[smem] + [vmem] * n_in,
        out_specs=out_specs,
        scratch_shapes=list(scratch),
        compiler_params=pltpu.CompilerParams(vmem_limit_bytes=24 * 2**20),
        cost_estimate=pl.CostEstimate(flops=flops, bytes_accessed=moved, transcendentals=0),
    )


def shards(a, row_perms, dest_rows, row_mask, col_mask):
    core = lax.axis_index("core")
    smem = pl.BlockSpec(memory_space=pltpu.SMEM)
    cut = a.reshape(SLOTS, NZ, 8, 2 * W)
    over = lax.ppermute(cut[:, 9:].transpose(1, 0, 2, 3), ("z", "core"), [(0, 1)])
    *pieces, own0 = lax.optimization_barrier(
        [jnp.where(core == 0, cut[:, z0], over[max(z1 - 9, 0)]) for z0, z1 in (*SENDS, (0, 0))]
    )
    got = []
    for (z0, z1), piece in zip(SENDS, pieces):
        pairs = ([(1, 2 * z1)] if z1 else []) + [(0, 2 * z0)]
        got.append(lax.ppermute(piece, ("z", "core"), pairs))

    out0, panel, last = call(
        route_kernel, (f32(NP, 9, 8, W), f32(14, 8, W), f32(2, 8, W)), 10, moved=2**20
    )(dest_rows, a[: 2 * W], own0, *got)
    out0, maps = lax.optimization_barrier((out0, (dest_rows, row_mask, col_mask)))
    passed = lax.ppermute(panel, "core", [(0, 1)])
    meta = pl.pallas_call(
        index_kernel,
        out_shape=jax.ShapeDtypeStruct((W,), jnp.int32),
        in_specs=[smem] * 3,
        out_specs=smem,
        scratch_shapes=[pltpu.SMEM((2, W), jnp.int32)],
    )(*maps)
    got0 = lax.all_to_all(out0, ("x", "y"), 0, 0, tiled=True)
    payload, chunk = call(pack_kernel, (f32(14, 8, W), f32(4, 8, W)), 3, moved=2**19)(
        meta, passed, last, got0
    )

    own = lax.all_gather(payload, "z", axis=0, tiled=False)
    oth = lax.ppermute(own, "core", [(0, 1), (1, 0)])

    send, plow, inv0, inv1, lsrc = call(
        factor_kernel,
        (f32(NP, H + 32, W), f32(SLOTS * W, W), f32(W, W), f32(W, W), f32(W, W)),
        3,
        scratch=(pltpu.VMEM((SLOTS * W, W), jnp.float32),),
        flops=5 * 10**8,
        moved=4 * 2**20,
    )(meta, own, oth, chunk)

    got1 = lax.all_to_all(send, ("x", "y"), 0, 0, tiled=True)
    lpan = call(panels_kernel, f32(SLOTS * W, 2 * W), 6, flops=5 * 10**8, moved=4 * 2**20)(
        meta, own, oth, plow, inv0, inv1, row_perms
    )
    got1, lpan = lax.optimization_barrier((got1, lpan))
    oth1 = lax.ppermute(got1[:, :H], "core", [(0, 1), (1, 0)])
    cur, kept = call(
        first_kernel, (f32(SLOTS * W, 2 * W), f32(W, 2 * W)), 5, flops=5 * 10**8, moved=3 * 2**20
    )(meta, a, got1, plow, lsrc, row_perms)
    schur = call(second_kernel, f32(SLOTS * W, 2 * W), 3, flops=3 * 10**8, moved=3 * 2**20)(
        meta, cur, oth1, kept
    )
    return schur, lpan


def solution(mesh):
    fine = Mesh(mesh.devices.reshape(4, 4, NZ, 2), ("x", "y", "z", "core"))
    placed = (P(("x", "y"), ("z", "core")), P(), P(), P(), P())
    return jax.shard_map(
        shards,
        mesh=fine,
        in_specs=placed,
        out_specs=(P(("x", "y"), ("z", "core")), P(("x", "y"), None)),
        check_vma=False,
    )
```

```python
import jax
import jax.numpy as jnp
from jax import lax
from jax.experimental import pallas as pl
from jax.experimental.pallas import tpu as pltpu
from jax.sharding import Mesh
from jax.sharding import PartitionSpec as P

SWEEPS = 3
W = 128
H = W // 2
NP = 16
NZ = 16
SLOTS = 8


def dot16(a, b):
    return jnp.dot(a, b, preferred_element_type=jnp.float32)


def split(x):
    high = x.astype(jnp.bfloat16)
    return high, (x - high.astype(jnp.float32)).astype(jnp.bfloat16)


def dot(a, b):
    left = jnp.concatenate(split(a), axis=1)
    right = jnp.concatenate(split(b), axis=1)
    both = dot16(left, jnp.concatenate([right, right], axis=0))
    n = b.shape[1]
    return both[:, :n] + both[:, n:]


def exact(x):
    high, mid = split(x)
    return high, mid, (x - high.astype(jnp.float32) - mid.astype(jnp.float32)).astype(jnp.bfloat16)


def order(perms, k):
    hit = lax.broadcasted_iota(jnp.int32, (W, W), 0) == perms[k : k + 1, :]
    return jnp.where(hit, 1.0, 0.0).astype(jnp.float32)


def reorder_rows(perms, k, x):
    move = order(perms, k).T.astype(jnp.bfloat16)
    high, mid, low = exact(x)
    return dot16(move, high) + (dot16(move, mid) + dot16(move, low))


def reorder_columns(perms, k, x):
    move = order(perms, k).astype(jnp.bfloat16)
    high, mid, low = exact(x)
    return dot16(high, move) + (dot16(mid, move) + dot16(low, move))


def index_kernel(dest, row_mask, col_mask, meta, src):
    me = lax.axis_index("x") * 4 + lax.axis_index("y")
    z = lax.axis_index("z")
    core = lax.axis_index("core")

    def invert(i, carry):
        src[0, dest[0, i]] = i
        src[1, dest[1, i]] = i
        return carry

    lax.fori_loop(0, W, invert, 0, unroll=8)

    def row_ok(k, i):
        return ((row_mask[k, i] == 1) & (i > k)).astype(jnp.int32)

    def col_ok(k, j):
        return ((col_mask[k, j] == 1) & (j > k)).astype(jnp.int32)

    head = src[0, 1]
    block = (z * 2 + core) * 2
    meta[0] = core
    meta[1] = (me == 0).astype(jnp.int32)
    meta[2] = col_ok(0, 1)
    meta[3] = row_ok(0, head)
    meta[4] = lax.shift_right_logical(head, 3)
    for k in range(2):
        for j in range(2):
            meta[64 + 2 * k + j] = col_ok(k, block + j)
    for slot in range(SLOTS):
        here = me * SLOTS + slot
        meta[8 + slot] = row_ok(0, here)
        meta[16 + slot] = row_ok(1, here)
        meta[24 + slot] = row_ok(0, src[0, here])
        meta[32 + slot] = lax.shift_right_logical(dest[1, here], 3)
        meta[40 + slot] = lax.shift_right_logical(src[1, here], 3)
        meta[56 + slot] = lax.shift_right_logical(src[0, here], 3)


def route_kernel(dest, a, own, *refs):
    got, (out, panel, last) = refs[:-3], refs[-3:]
    me = lax.axis_index("x") * 4 + lax.axis_index("y")
    root = (lax.axis_index("z") == 0) & (lax.axis_index("core") == 0)
    share = own[...] * root.astype(jnp.float32)
    for ref in got:
        share = share + ref[...]
    for slot in range(SLOTS):
        left, right = share[slot, :, :W], share[slot, :, W:]
        out[lax.shift_right_logical(dest[0, me * SLOTS + slot], 3), 0] = left
        if slot < 7:
            panel[slot] = left
            panel[7 + slot] = right
        else:
            last[0] = left
            last[1] = right
        if slot < 2:
            out[:, 1 + 2 * slot] = jnp.broadcast_to(left[None], (NP, 8, W))
            out[:, 2 + 2 * slot] = jnp.broadcast_to(right[None], (NP, 8, W))
    rows = a[: 2 * W].reshape(NP, 2, 8, 2 * W)
    out[:, 5:7] = rows[..., :W]
    out[:, 7:9] = rows[..., W:]


def pack_kernel(meta, passed, last, got, out, chunk):
    chunk[...] = got[0, 5:9]

    @pl.when(meta[0] == 1)
    def _():
        out[...] = passed[...]

    @pl.when(meta[0] == 0)
    def _():
        out[:2] = last[...]
        for slot in range(SLOTS):
            out[2 + slot] = got[meta[56 + slot], 0]
        out[10:12] = got[0, 1:3]
        out[12] = got[meta[4], 3]
        out[13] = got[0, 4]


def refine(block):
    row = lax.broadcasted_iota(jnp.int32, (W, W), 0)
    col = lax.broadcasted_iota(jnp.int32, (W, W), 1)
    one = jnp.where(row == col, 1.0, 0.0).astype(jnp.float32)
    scale = W * (jnp.mean(block * block) + 1e-6)
    approx = block.T / scale
    rest = one - dot(block, approx)
    for sweep in range(SWEEPS):
        approx = approx + dot(approx, rest)
        if sweep + 1 < SWEEPS:
            rest = dot(rest, rest)
    return approx


def tile(ref, t):
    return ref[:, t].reshape(W, W)


def flagged(meta, block, base):
    return jnp.concatenate(
        [block[s * W : (s + 1) * W] * meta[base + s].astype(jnp.float32) for s in range(SLOTS)], axis=0
    )


def lower1(meta, head, panel, ext0, inv1):
    kept01 = tile(head, 11) * meta[2].astype(jnp.float32)
    col1 = jnp.concatenate([tile(panel, 7 + s) for s in range(7)] + [tile(head, 1)], axis=0)
    return flagged(meta, dot(col1 - dot(ext0, kept01), inv1[...]), 16)


def factor(meta, head, panel, send, plow, inv0, inv1, lsrc, low1):
    inv = refine(tile(head, 10))
    inv0[...] = inv
    kept01 = tile(head, 11) * meta[2].astype(jnp.float32)
    low_src = dot(tile(head, 12), inv) * meta[3].astype(jnp.float32)
    lsrc[...] = low_src
    inv1[...] = refine(tile(head, 13) - dot(low_src, kept01))
    ext0 = jnp.concatenate([tile(head, 2 + s) for s in range(SLOTS)], axis=0)
    ext0 = flagged(meta, dot(ext0, inv), 24)
    plow[...] = ext0
    low1[...] = lower1(meta, head, panel, ext0, inv1)
    for slot in range(SLOTS):
        half = pl.ds(pl.multiple_of(slot * W + meta[0] * H, H), H)
        send[meta[32 + slot], :H] = low1[half, :]


def factor_kernel(meta, own, oth, chunk, send, *refs):
    @pl.when(meta[0] == 0)
    def _():
        factor(meta, own, oth, send, *refs)

    @pl.when(meta[0] == 1)
    def _():
        factor(meta, oth, own, send, *refs)

    send[:, H:] = jnp.broadcast_to(chunk[...].reshape(1, 32, W), (NP, 32, W))


def panels_kernel(meta, own, oth, plow, inv0, inv1, perms, lpan):
    def write(head, panel):
        col0 = jnp.concatenate([tile(panel, s) for s in range(7)] + [tile(head, 0)], axis=0)
        lpan[:, :W] = flagged(meta, dot(col0, reorder_columns(perms, 0, inv0[...])), 8)
        low = lower1(meta, head, panel, plow[...], inv1)
        lpan[:, W:] = reorder_columns(perms, 1, low)

    @pl.when(meta[0] == 0)
    def _():
        write(own, oth)

    @pl.when(meta[0] == 1)
    def _():
        write(oth, own)


def subtract(meta, half_of, kept, out, half):
    low = jnp.concatenate([half_of(meta[40 + slot]) for slot in range(SLOTS)], axis=0)
    prod = dot(low, kept[...])
    for slot in range(SLOTS):
        here = pl.ds(pl.multiple_of(slot * W + half * H, H), H)
        out[here, :] = out[here, :] - prod[slot * H : (slot + 1) * H]


def first_kernel(meta, a, got, plow, lsrc, perms, cur, kept):
    def masked(block, k):
        return jnp.concatenate(
            [block[:, j * W : (j + 1) * W] * meta[64 + 2 * k + j].astype(jnp.float32) for j in range(2)],
            axis=1,
        )

    rows = jnp.concatenate(
        [got[:, H : H + 16].reshape(2 * W, W), got[:, H + 16 :].reshape(2 * W, W)], axis=1
    )
    kept0 = masked(rows[:W], 0)
    next1 = rows[W:] - dot(lsrc[...], kept0)
    kept[...] = masked(next1, 1)
    prod = dot(plow[...], kept0)
    cur[...] = a[...] - prod

    @pl.when(meta[1] == 1)
    def _():
        cur[:W] = reorder_rows(perms, 0, rows[:W]) - prod[:W]
        cur[W : 2 * W] = reorder_rows(perms, 1, next1)

    subtract(meta, lambda dev: got[dev, :H], kept, cur, meta[0])


def second_kernel(meta, cur, oth, kept, out):
    out[...] = cur[...]
    subtract(meta, lambda dev: oth[dev], kept, out, 1 - meta[0])


def f32(*shape):
    return jax.ShapeDtypeStruct(shape, jnp.float32)


def call(kernel, out_shape, n_in, scratch=(), flops=0, moved=0):
    smem = pl.BlockSpec(memory_space=pltpu.SMEM)
    vmem = pl.BlockSpec(memory_space=pltpu.VMEM)
    out_specs = [vmem] * len(out_shape) if isinstance(out_shape, tuple) else vmem
    return pl.pallas_call(
        kernel,
        out_shape=out_shape,
        in_specs=[smem] + [vmem] * n_in,
        out_specs=out_specs,
        scratch_shapes=list(scratch),
        compiler_params=pltpu.CompilerParams(vmem_limit_bytes=24 * 2**20),
        cost_estimate=pl.CostEstimate(flops=flops, bytes_accessed=moved, transcendentals=0),
    )


def shards(a, row_perms, dest_rows, row_mask, col_mask):
    core = lax.axis_index("core")
    smem = pl.BlockSpec(memory_space=pltpu.SMEM)
    cut = a.reshape(SLOTS, NZ, 8, 2 * W)
    over = lax.ppermute(cut[:, 8:].transpose(1, 0, 2, 3), ("z", "core"), [(0, 1)])
    pieces = [jnp.where(core == 0, cut[:, step % 8], over[8 - step]) for step in range(1, 9)]
    pieces = lax.optimization_barrier(pieces)
    got = []
    for step in range(1, 9):
        pairs = [(1, 2 * (NZ - step))]
        if step < 8:
            pairs.append((0, 2 * step))
        got.append(lax.ppermute(pieces[step - 1], ("z", "core"), pairs))

    out0, panel, last = call(
        route_kernel, (f32(NP, 9, 8, W), f32(14, 8, W), f32(2, 8, W)), 10, moved=2**20
    )(dest_rows, a[: 2 * W], pieces[7], *got)
    out0, maps = lax.optimization_barrier((out0, (dest_rows, row_mask, col_mask)))
    passed = lax.ppermute(panel, "core", [(0, 1)])
    meta = pl.pallas_call(
        index_kernel,
        out_shape=jax.ShapeDtypeStruct((W,), jnp.int32),
        in_specs=[smem] * 3,
        out_specs=smem,
        scratch_shapes=[pltpu.SMEM((2, W), jnp.int32)],
    )(*maps)
    got0 = lax.all_to_all(out0, ("x", "y"), 0, 0, tiled=True)
    payload, chunk = call(pack_kernel, (f32(14, 8, W), f32(4, 8, W)), 3, moved=2**19)(
        meta, passed, last, got0
    )

    own = lax.all_gather(payload, "z", axis=0, tiled=False)
    oth = lax.ppermute(own, "core", [(0, 1), (1, 0)])

    send, plow, inv0, inv1, lsrc = call(
        factor_kernel,
        (f32(NP, H + 32, W), f32(SLOTS * W, W), f32(W, W), f32(W, W), f32(W, W)),
        3,
        scratch=(pltpu.VMEM((SLOTS * W, W), jnp.float32),),
        flops=5 * 10**8,
        moved=4 * 2**20,
    )(meta, own, oth, chunk)

    got1 = lax.all_to_all(send, ("x", "y"), 0, 0, tiled=True)
    lpan = call(panels_kernel, f32(SLOTS * W, 2 * W), 6, flops=5 * 10**8, moved=4 * 2**20)(
        meta, own, oth, plow, inv0, inv1, row_perms
    )
    got1, lpan = lax.optimization_barrier((got1, lpan))
    oth1 = lax.ppermute(got1[:, :H], "core", [(0, 1), (1, 0)])
    cur, kept = call(
        first_kernel, (f32(SLOTS * W, 2 * W), f32(W, 2 * W)), 5, flops=5 * 10**8, moved=3 * 2**20
    )(meta, a, got1, plow, lsrc, row_perms)
    schur = call(second_kernel, f32(SLOTS * W, 2 * W), 3, flops=3 * 10**8, moved=3 * 2**20)(
        meta, cur, oth1, kept
    )
    return schur, lpan


def solution(mesh):
    fine = Mesh(mesh.devices.reshape(4, 4, NZ, 2), ("x", "y", "z", "core"))
    placed = (P(("x", "y"), ("z", "core")), P(), P(), P(), P())
    return jax.shard_map(
        shards,
        mesh=fine,
        in_specs=placed,
        out_specs=(P(("x", "y"), ("z", "core")), P(("x", "y"), None)),
        check_vma=False,
    )
```

```python
import jax
import jax.numpy as jnp
from jax import lax
from jax.experimental import pallas as pl
from jax.experimental.pallas import tpu as pltpu
from jax.sharding import Mesh
from jax.sharding import PartitionSpec as P

SWEEPS = 3
W = 128
H = W // 2
NP = 16
NZ = 16
SLOTS = 8


def dot16(a, b):
    return jnp.dot(a, b, preferred_element_type=jnp.float32)


def split(x):
    high = x.astype(jnp.bfloat16)
    return high, (x - high.astype(jnp.float32)).astype(jnp.bfloat16)


def dot(a, b):
    left = jnp.concatenate(split(a), axis=1)
    right = jnp.concatenate(split(b), axis=1)
    both = dot16(left, jnp.concatenate([right, right], axis=0))
    n = b.shape[1]
    return both[:, :n] + both[:, n:]


def exact(x):
    high, mid = split(x)
    return high, mid, (x - high.astype(jnp.float32) - mid.astype(jnp.float32)).astype(jnp.bfloat16)


def order(perms, k):
    hit = lax.broadcasted_iota(jnp.int32, (W, W), 0) == perms[k : k + 1, :]
    return jnp.where(hit, 1.0, 0.0).astype(jnp.float32)


def reorder_rows(perms, k, x):
    move = order(perms, k).T.astype(jnp.bfloat16)
    high, mid, low = exact(x)
    return dot16(move, high) + (dot16(move, mid) + dot16(move, low))


def reorder_columns(perms, k, x):
    move = order(perms, k).astype(jnp.bfloat16)
    high, mid, low = exact(x)
    return dot16(high, move) + (dot16(mid, move) + dot16(low, move))


def index_kernel(dest, row_mask, col_mask, meta, src):
    me = lax.axis_index("x") * 4 + lax.axis_index("y")
    z = lax.axis_index("z")
    core = lax.axis_index("core")

    def invert(i, carry):
        src[0, dest[0, i]] = i
        src[1, dest[1, i]] = i
        return carry

    lax.fori_loop(0, W, invert, 0, unroll=8)

    def row_ok(k, i):
        return ((row_mask[k, i] == 1) & (i > k)).astype(jnp.int32)

    def col_ok(k, j):
        return ((col_mask[k, j] == 1) & (j > k)).astype(jnp.int32)

    head = src[0, 1]
    block = (z * 2 + core) * 2
    meta[0] = core
    meta[1] = (me == 0).astype(jnp.int32)
    meta[2] = col_ok(0, 1)
    meta[3] = row_ok(0, head)
    meta[4] = lax.shift_right_logical(head, 3)
    for k in range(2):
        for j in range(2):
            meta[64 + 2 * k + j] = col_ok(k, block + j)
    for slot in range(SLOTS):
        here = me * SLOTS + slot
        meta[8 + slot] = row_ok(0, here)
        meta[16 + slot] = row_ok(1, here)
        meta[24 + slot] = row_ok(0, src[0, here])
        meta[32 + slot] = lax.shift_right_logical(dest[1, here], 3)
        meta[40 + slot] = lax.shift_right_logical(src[1, here], 3)
        meta[56 + slot] = lax.shift_right_logical(src[0, here], 3)


def route_kernel(dest, a, own, *refs):
    got, (out, panel, last) = refs[:-3], refs[-3:]
    me = lax.axis_index("x") * 4 + lax.axis_index("y")
    root = (lax.axis_index("z") == 0) & (lax.axis_index("core") == 0)
    share = own[...] * root.astype(jnp.float32)
    for ref in got:
        share = share + ref[...]
    for slot in range(SLOTS):
        left, right = share[slot, :, :W], share[slot, :, W:]
        out[lax.shift_right_logical(dest[0, me * SLOTS + slot], 3), 0] = left
        if slot < 7:
            panel[slot] = left
            panel[7 + slot] = right
        else:
            last[0] = left
            last[1] = right
        if slot < 2:
            out[:, 1 + 2 * slot] = jnp.broadcast_to(left[None], (NP, 8, W))
            out[:, 2 + 2 * slot] = jnp.broadcast_to(right[None], (NP, 8, W))
    rows = a[: 2 * W].reshape(NP, 2, 8, 2 * W)
    out[:, 5:7] = rows[..., :W]
    out[:, 7:9] = rows[..., W:]


def pack_kernel(meta, passed, last, got, out, chunk):
    chunk[...] = got[0, 5:9]

    @pl.when(meta[0] == 1)
    def _():
        out[...] = passed[...]

    @pl.when(meta[0] == 0)
    def _():
        out[:2] = last[...]
        for slot in range(SLOTS):
            out[2 + slot] = got[meta[56 + slot], 0]
        out[10:12] = got[0, 1:3]
        out[12] = got[meta[4], 3]
        out[13] = got[0, 4]


def refine(block):
    row = lax.broadcasted_iota(jnp.int32, (W, W), 0)
    col = lax.broadcasted_iota(jnp.int32, (W, W), 1)
    one = jnp.where(row == col, 1.0, 0.0).astype(jnp.float32)
    scale = W * (jnp.mean(block * block) + 1e-6)
    approx = block.T / scale
    rest = one - dot(block, approx)
    for sweep in range(SWEEPS):
        approx = approx + dot(approx, rest)
        if sweep + 1 < SWEEPS:
            rest = dot(rest, rest)
    return approx


def tile(ref, t):
    return ref[:, t].reshape(W, W)


def flagged(meta, block, base):
    return jnp.concatenate(
        [block[s * W : (s + 1) * W] * meta[base + s].astype(jnp.float32) for s in range(SLOTS)], axis=0
    )


def lower1(meta, head, panel, ext0, inv1):
    kept01 = tile(head, 11) * meta[2].astype(jnp.float32)
    col1 = jnp.concatenate([tile(panel, 7 + s) for s in range(7)] + [tile(head, 1)], axis=0)
    return flagged(meta, dot(col1 - dot(ext0, kept01), inv1[...]), 16)


def factor(meta, head, panel, send, plow, inv0, inv1, lsrc, low1):
    inv = refine(tile(head, 10))
    inv0[...] = inv
    kept01 = tile(head, 11) * meta[2].astype(jnp.float32)
    low_src = dot(tile(head, 12), inv) * meta[3].astype(jnp.float32)
    lsrc[...] = low_src
    inv1[...] = refine(tile(head, 13) - dot(low_src, kept01))
    ext0 = jnp.concatenate([tile(head, 2 + s) for s in range(SLOTS)], axis=0)
    ext0 = flagged(meta, dot(ext0, inv), 24)
    plow[...] = ext0
    low1[...] = lower1(meta, head, panel, ext0, inv1)
    for slot in range(SLOTS):
        half = pl.ds(pl.multiple_of(slot * W + meta[0] * H, H), H)
        send[meta[32 + slot], :H] = low1[half, :]


def factor_kernel(meta, own, oth, chunk, send, *refs):
    @pl.when(meta[0] == 0)
    def _():
        factor(meta, own, oth, send, *refs)

    @pl.when(meta[0] == 1)
    def _():
        factor(meta, oth, own, send, *refs)

    send[:, H:] = jnp.broadcast_to(chunk[...].reshape(1, 32, W), (NP, 32, W))


def panels_kernel(meta, own, oth, plow, inv0, inv1, perms, lpan):
    def write(head, panel):
        col0 = jnp.concatenate([tile(panel, s) for s in range(7)] + [tile(head, 0)], axis=0)
        lpan[:, :W] = flagged(meta, dot(col0, reorder_columns(perms, 0, inv0[...])), 8)
        low = lower1(meta, head, panel, plow[...], inv1)
        lpan[:, W:] = reorder_columns(perms, 1, low)

    @pl.when(meta[0] == 0)
    def _():
        write(own, oth)

    @pl.when(meta[0] == 1)
    def _():
        write(oth, own)


def subtract(meta, half_of, kept, out, half):
    low = jnp.concatenate([half_of(meta[40 + slot]) for slot in range(SLOTS)], axis=0)
    prod = dot(low, kept[...])
    for slot in range(SLOTS):
        here = pl.ds(pl.multiple_of(slot * W + half * H, H), H)
        out[here, :] = out[here, :] - prod[slot * H : (slot + 1) * H]


def first_kernel(meta, a, got, plow, lsrc, perms, cur, kept):
    def masked(block, k):
        return jnp.concatenate(
            [block[:, j * W : (j + 1) * W] * meta[64 + 2 * k + j].astype(jnp.float32) for j in range(2)],
            axis=1,
        )

    rows = jnp.concatenate(
        [got[:, H : H + 16].reshape(2 * W, W), got[:, H + 16 :].reshape(2 * W, W)], axis=1
    )
    kept0 = masked(rows[:W], 0)
    next1 = rows[W:] - dot(lsrc[...], kept0)
    kept[...] = masked(next1, 1)
    prod = dot(plow[...], kept0)
    cur[...] = a[...] - prod

    @pl.when(meta[1] == 1)
    def _():
        cur[:W] = reorder_rows(perms, 0, rows[:W]) - prod[:W]
        cur[W : 2 * W] = reorder_rows(perms, 1, next1)

    subtract(meta, lambda dev: got[dev, :H], kept, cur, meta[0])


def second_kernel(meta, cur, oth, kept, out):
    out[...] = cur[...]
    subtract(meta, lambda dev: oth[dev], kept, out, 1 - meta[0])


def f32(*shape):
    return jax.ShapeDtypeStruct(shape, jnp.float32)


def call(kernel, out_shape, n_in, scratch=(), flops=0, moved=0):
    smem = pl.BlockSpec(memory_space=pltpu.SMEM)
    vmem = pl.BlockSpec(memory_space=pltpu.VMEM)
    out_specs = [vmem] * len(out_shape) if isinstance(out_shape, tuple) else vmem
    return pl.pallas_call(
        kernel,
        out_shape=out_shape,
        in_specs=[smem] + [vmem] * n_in,
        out_specs=out_specs,
        scratch_shapes=list(scratch),
        compiler_params=pltpu.CompilerParams(vmem_limit_bytes=24 * 2**20),
        cost_estimate=pl.CostEstimate(flops=flops, bytes_accessed=moved, transcendentals=0),
    )


def shards(a, row_perms, dest_rows, row_mask, col_mask):
    core = lax.axis_index("core")
    smem = pl.BlockSpec(memory_space=pltpu.SMEM)
    cut = a.reshape(SLOTS, NZ, 8, 2 * W)
    over = lax.ppermute(cut[:, 9:].transpose(1, 0, 2, 3), ("z", "core"), [(0, 1)])
    pieces = [jnp.where(core == 0, cut[:, step % 9], over[max(7 - step, 0)]) for step in range(1, 10)]
    pieces = lax.optimization_barrier(pieces)
    got = []
    for step in range(1, 9):
        pairs = [(0, 2 * step)]
        if step < 8:
            pairs.append((1, 2 * (NZ - step)))
        got.append(lax.ppermute(pieces[step - 1], ("z", "core"), pairs))

    out0, panel, last = call(
        route_kernel, (f32(NP, 9, 8, W), f32(14, 8, W), f32(2, 8, W)), 10, moved=2**20
    )(dest_rows, a[: 2 * W], pieces[8], *got)
    out0, maps = lax.optimization_barrier((out0, (dest_rows, row_mask, col_mask)))
    passed = lax.ppermute(panel, "core", [(0, 1)])
    meta = pl.pallas_call(
        index_kernel,
        out_shape=jax.ShapeDtypeStruct((W,), jnp.int32),
        in_specs=[smem] * 3,
        out_specs=smem,
        scratch_shapes=[pltpu.SMEM((2, W), jnp.int32)],
    )(*maps)
    got0 = lax.all_to_all(out0, ("x", "y"), 0, 0, tiled=True)
    payload, chunk = call(pack_kernel, (f32(14, 8, W), f32(4, 8, W)), 3, moved=2**19)(
        meta, passed, last, got0
    )

    own = lax.all_gather(payload, "z", axis=0, tiled=False)
    oth = lax.ppermute(own, "core", [(0, 1), (1, 0)])

    send, plow, inv0, inv1, lsrc = call(
        factor_kernel,
        (f32(NP, H + 32, W), f32(SLOTS * W, W), f32(W, W), f32(W, W), f32(W, W)),
        3,
        scratch=(pltpu.VMEM((SLOTS * W, W), jnp.float32),),
        flops=5 * 10**8,
        moved=4 * 2**20,
    )(meta, own, oth, chunk)

    got1 = lax.all_to_all(send, ("x", "y"), 0, 0, tiled=True)
    lpan = call(panels_kernel, f32(SLOTS * W, 2 * W), 6, flops=5 * 10**8, moved=4 * 2**20)(
        meta, own, oth, plow, inv0, inv1, row_perms
    )
    got1, lpan = lax.optimization_barrier((got1, lpan))
    oth1 = lax.ppermute(got1[:, :H], "core", [(0, 1), (1, 0)])
    cur, kept = call(
        first_kernel, (f32(SLOTS * W, 2 * W), f32(W, 2 * W)), 5, flops=5 * 10**8, moved=3 * 2**20
    )(meta, a, got1, plow, lsrc, row_perms)
    schur = call(second_kernel, f32(SLOTS * W, 2 * W), 3, flops=3 * 10**8, moved=3 * 2**20)(
        meta, cur, oth1, kept
    )
    return schur, lpan


def solution(mesh):
    fine = Mesh(mesh.devices.reshape(4, 4, NZ, 2), ("x", "y", "z", "core"))
    placed = (P(("x", "y"), ("z", "core")), P(), P(), P(), P())
    return jax.shard_map(
        shards,
        mesh=fine,
        in_specs=placed,
        out_specs=(P(("x", "y"), ("z", "core")), P(("x", "y"), None)),
        check_vma=False,
    )
```
